128 devices in a mesh: pool: 128 (over x, z, y, core).
Axes of the slice: x: 4, y: 4, z: 4, core: 2. Of those that a mesh axis runs over, the one named last changes fastest.
Arguments:
- queries: bfloat16 [128, 2, 3584], P('pool'), may hold values from -120 to 120
- kv_pool: bfloat16 [4096, 256, 2, 512], P('pool'), may hold values from -6 to 6
- lengths: int32 [128], P('pool'), may hold values from 1 to 8190, 524288 in all
- block_table: int32 [4096], P('pool'), may hold values from 0 to 4095, as said below
Outputs:
- attended: bfloat16 [128, 2, 3584], P('pool')
The draws below stay inside these ranges and needn't reach their ends.
Inputs may be any that keep to these rules, and one draw needn't show every extreme that they name: `block_table`: a permutation of the pool blocks; with the requests numbered in groups of 1 per owner index o and G groups, the entry at place j of the 32 entries of group o is a block numbered from ((o + s_j) mod G) * 32 to that + 31, where s_j = (j * G) // 32, except s_0 = 1 when G > 32. The pool holds positions 0 to lengths + 1 of each request.
All inputs are finite; a program needn't handle non-finite values. No bound on the sum of `lengths` on one device may be relied on, other than what follows from the above.
Results may differ from the reference program's by a relative error of at most 0.0095.
Values may be sent and summed in bfloat16 or wider, within the bound.
No kernel may reach another device: no remote copies, remote signals or barrier semaphores. Data moves between devices by JAX's collectives and lax.ppermute only.
A program may use at most 192 MiB of HBM per device.

```python
import math
import jax
import jax.numpy as jnp
import numpy as np
from jax import lax

KVH = 4
GROUP = 7
HEAD = 128
BLOCK = 256
MAXBLK = 32
REQ_DEV = 1
REQUESTS = 128
POOL_DEV = 32
POOL = 4096


def draw_queries(key, part):
    key = jax.random.fold_in(key, 11)
    first_key = jax.random.fold_in(key, 0)
    drawn_rows = jnp.clip(jax.random.normal(first_key, (REQUESTS, 2, KVH, GROUP, HEAD), jnp.float32), -6.0, 6.0)
    return drawn_rows.reshape(REQUESTS, 2, KVH * GROUP * HEAD).astype(jnp.bfloat16)


def draw_kv_pool(key, part):
    key = jax.random.fold_in(key, 23)
    first_key = jax.random.fold_in(key, 0)
    third_key = jax.random.fold_in(key, 2)
    cache_keys = jnp.clip(jax.random.normal(first_key, (POOL, BLOCK, KVH, HEAD), jnp.float32), -6.0, 6.0)
    cache_values = jnp.clip(jax.random.normal(third_key, (POOL, BLOCK, KVH, HEAD), jnp.float32), -6.0, 6.0)
    stacked = jnp.stack([cache_keys, cache_values], axis=2)
    return stacked.reshape(POOL, BLOCK, 2, KVH * HEAD).astype(jnp.bfloat16)


def draw_block_table(key, part):
    key = jax.random.fold_in(key, 37)
    owners = REQUESTS // REQ_DEV
    first_step = 1 if owners > POOL_DEV else 0
    device_keys = jax.random.split(key, owners)
    orders = jax.vmap(lambda one_key: jax.random.permutation(one_key, jnp.arange(POOL_DEV, dtype=jnp.int32)))(device_keys)
    owner_ids = jnp.arange(owners, dtype=jnp.int32)[:, None]
    places = jnp.arange(POOL_DEV, dtype=jnp.int32)[None, :]
    steps_away = jnp.where(places == 0, first_step, places * owners // POOL_DEV).astype(jnp.int32)
    holders = (owner_ids + steps_away) % owners
    slots = orders[holders, jnp.broadcast_to(places, holders.shape)]
    return (holders * POOL_DEV + slots).reshape(REQUESTS * MAXBLK).astype(jnp.int32)


def split_up(count, total, reach, slope):
    portions = [(1 << 20) // math.isqrt(grade ** slope) + 1 for grade in range(2, count + 1)]
    spare, given = total - reach - (count - 1), [1] * (count - 1)
    while spare > 0:
        free = [i for i in range(count - 1) if given[i] < reach]
        whole, remaining = sum([portions[i] for i in free]), spare
        for i in free:
            more = min(reach - given[i], max(1, remaining * portions[i] // whole), spare)
            given[i] = given[i] + more
            spare = spare - more
    return np.array([reach] + given)


def ragged(key, amount, total, reach, lean):
    if amount == 2:
        one = jax.random.randint(key, (), max(1, total - reach), min(reach, total - 1) + 1)
        return jnp.stack([one, total - one])
    sizes = jnp.asarray(split_up(amount, total, reach, lean), jnp.int32)
    pairs = (amount - 1) // 2
    giver, receiver = sizes[1:1 + 2 * pairs:2], sizes[2:2 + 2 * pairs:2]
    slack = jnp.minimum(giver - 1, reach - receiver)
    moved = jax.random.randint(jax.random.fold_in(key, 1), (pairs,), 0, 1 << 20) % (slack + 1)
    sizes = sizes.at[1:1 + 2 * pairs:2].set(giver - moved).at[2:2 + 2 * pairs:2].set(receiver + moved)
    return sizes[jax.random.permutation(jax.random.fold_in(key, 2), amount)]


def setup_inputs(seed: int = 0) -> dict:
    streams_of = jax.random.split(jax.random.key(seed), 5)
    queries = draw_queries(jax.random.fold_in(streams_of[4], 71), 0)
    kv_pool = draw_kv_pool(jax.random.fold_in(streams_of[4], 71), 0)
    lengths = ragged(streams_of[2], REQUESTS, REQUESTS * (MAXBLK * BLOCK // 2), MAXBLK * BLOCK - 2, 2).astype(jnp.int32)
    block_table = draw_block_table(jax.random.fold_in(streams_of[4], 71), 0)
    return dict(queries=queries, kv_pool=kv_pool, lengths=lengths, block_table=block_table)


def reference(queries, kv_pool, lengths, block_table):
    table_rows = block_table.reshape(REQUESTS, MAXBLK)
    score_scale = 1.0 / (HEAD ** 0.5)

    def attend_one(request_data):
        request_query, length, blocks = request_data
        gathered = kv_pool[blocks]
        cache_keys = gathered[:, :, 0, :].reshape(MAXBLK * BLOCK, KVH, HEAD).astype(jnp.float32)
        cache_values = gathered[:, :, 1, :].reshape(MAXBLK * BLOCK, KVH, HEAD).astype(jnp.float32)
        query_rows = request_query.reshape(2, KVH, GROUP, HEAD).astype(jnp.float32)
        scores = jnp.einsum("tkgd,pkd->tkgp", query_rows, cache_keys, precision=lax.Precision.HIGHEST) * score_scale
        positions = jnp.arange(MAXBLK * BLOCK, dtype=jnp.int32)
        visible_end = length + 1 + jnp.arange(2, dtype=jnp.int32)
        visible = positions[None, :] < visible_end[:, None]
        scores = jnp.where(visible[:, None, None, :], scores, -jnp.inf)
        row_max = jnp.max(scores, axis=-1, keepdims=True)
        unscaled = jnp.exp(scores - row_max)
        total = jnp.sum(unscaled, axis=-1)
        weights = lax.optimization_barrier(unscaled.astype(jnp.bfloat16)).astype(jnp.float32)
        numerator = jnp.einsum("tkgp,pkd->tkgd", weights, cache_values, precision=lax.Precision.HIGHEST)
        return (numerator / total[..., None]).reshape(2, KVH * GROUP * HEAD).astype(jnp.bfloat16)

    return lax.map(attend_one, (queries, lengths, table_rows))
```

```python
import jax
import jax.numpy as jnp
from jax import lax
from jax.experimental import pallas as pl
from jax.experimental.pallas import tpu as pltpu
from jax.sharding import PartitionSpec as P

KVH = 4
GROUP = 7
HEAD = 128
BLOCK = 256
PLACES = 32
DEVICES = 128
STRIDE = DEVICES // PLACES
ROWS = 2 * GROUP
PAD = 16
QROWS = KVH * ROWS
PROWS = KVH * PAD
CHUNK = PROWS + PAD
LINES = BLOCK * KVH * 2
TILE = 256
META = ROWS
UNROLL = 2
LOG2_SCALE = 1.4426950408889634 / HEAD**0.5
HIDDEN = -(2.0**120)
GROUPS = [[STRIDE * i + r for i in range(PLACES)] for r in range(STRIDE)]
NEXT = [(d, (d + 1) % DEVICES) for d in range(DEVICES)]
PREVIOUS = [((d + 1) % DEVICES, d) for d in range(DEVICES)]


def my_member():
    return lax.axis_index("pool") // STRIDE


def iota(shape, dim):
    return lax.broadcasted_iota(jnp.int32, shape, dim)


def pad_matrix(shape, padded_dim):
    padded, plain = iota(shape, padded_dim), iota(shape, 1 - padded_dim)
    hit = (padded % PAD < ROWS) & (padded // PAD * ROWS + padded % PAD == plain)
    return jnp.where(hit, 1.0, 0.0).astype(jnp.bfloat16)


def split3(x):
    hi = x.astype(jnp.bfloat16).astype(jnp.float32)
    rest = x - hi
    mid = rest.astype(jnp.bfloat16).astype(jnp.float32)
    return hi, mid, rest - mid


def pack_kernel(length_ref, table_ref, query_ref, sent_ref, first_ref):
    member = my_member()
    padded = jnp.dot(
        pad_matrix((PROWS, QROWS), 0), query_ref[...], preferred_element_type=jnp.float32
    )
    length = length_ref[0]
    row, lane = iota((PAD, HEAD), 0), iota((PAD, HEAD), 1)
    is_meta = row == META
    length_lanes = jnp.where(lane == 1, length // 128, jnp.where(lane == 2, length % 128, 0))
    head = padded[:PAD]
    rest = padded[PAD:].astype(jnp.bfloat16)

    def chunk_head(place):
        slot = table_ref[place] % PLACES
        meta = jnp.where(lane == 0, slot, length_lanes).astype(jnp.float32)
        return jnp.where(is_meta, meta, head).astype(jnp.bfloat16)

    for i in range(PLACES):
        sent_ref[i, :PAD, :] = chunk_head(lax.rem(i + PLACES - member, PLACES))
        sent_ref[i, PAD:, :] = rest
    first_ref[:PAD, :] = chunk_head(0)
    first_ref[PAD:, :] = rest


def attend_kernel(
    held_ref, first_ref, lines_ref, out_ref, out_first_ref, meta_vmem, meta_smem, todo, meta_sem
):
    member = my_member()
    meta = jnp.where(
        iota((PLACES, PAD, HEAD), 1) == META, held_ref[:, :PAD, :].astype(jnp.float32), 0.0
    )
    meta = jnp.sum(meta, axis=1)
    meta_first = jnp.sum(
        jnp.where(iota((PAD, HEAD), 0) == META, first_ref[:PAD, :].astype(jnp.float32), 0.0),
        axis=0,
        keepdims=True,
    )
    meta = jnp.where(iota((PLACES, HEAD), 0) == member, meta_first, meta)
    meta_vmem[...] = meta.astype(jnp.int32)
    copy = pltpu.make_async_copy(meta_vmem, meta_smem, meta_sem)
    copy.start()

    lane = iota((PAD, HEAD), 1)
    head_of_lane = lane % 8 // 2
    token = iota((PAD, HEAD), 0) % 2
    value_of = [
        jnp.where(lane % 8 == 2 * k + 1, 1.0, 0.0).astype(jnp.bfloat16) for k in range(KVH)
    ]

    def meta_rows(peak, total):
        parts = (*split3(peak), *split3(total))
        rows = jnp.zeros_like(peak)
        for g, part in enumerate(parts):
            rows = jnp.where(lane // 8 == g, part, rows)
        return rows.astype(jnp.bfloat16)

    no_numer = jnp.zeros((PROWS, HEAD), jnp.bfloat16)
    no_meta = meta_rows(jnp.full((PAD, HEAD), HIDDEN), jnp.zeros((PAD, HEAD)))
    for i in range(PLACES):
        out_ref[i, :PROWS, :] = no_numer
        out_ref[i, PROWS:, :] = no_meta
    copy.wait()

    def place_of(i):
        return lax.rem(member + PLACES - i, PLACES)

    def length_of(i):
        return meta_smem[i, 1] * 128 + meta_smem[i, 2]

    def note(i, count):
        seen = place_of(i) * BLOCK < length_of(i) + 2

        @pl.when(seen)
        def _():
            todo[count] = i

        return count + seen.astype(jnp.int32)

    count = lax.fori_loop(0, PLACES, note, jnp.int32(0))

    def attend(i):
        slot = meta_smem[i, 0]
        query = jnp.where(i == member, first_ref[...], held_ref[i])
        limit = 8 * (length_of(i) + 1 - place_of(i) * BLOCK + token)
        scores = []
        for n in range(LINES // TILE):
            tile = lines_ref[slot, n * TILE : (n + 1) * TILE, :]
            every = lax.dot_general(
                query, tile, (((1,), (1,)), ((), ())), preferred_element_type=jnp.float32
            )
            for half in range(TILE // HEAD):
                part = every[:, half * HEAD : (half + 1) * HEAD]
                own = part[(KVH - 1) * PAD :]
                for k in range(KVH - 1):
                    own = jnp.where(head_of_lane == k, part[k * PAD : (k + 1) * PAD], own)
                at = n * TILE + half * HEAD
                scores.append(jnp.where(lane < limit - at, own, HIDDEN))
        peak = scores[0]
        for part in scores[1:]:
            peak = jnp.maximum(peak, part)
        for shift in (8, 16, 32, 64):
            peak = jnp.maximum(peak, pltpu.roll(peak, shift, 1))
        total = jnp.zeros((PAD, HEAD), jnp.float32)
        numer = jnp.zeros((PROWS, HEAD), jnp.float32)
        for n in range(LINES // TILE):
            tile = lines_ref[slot, n * TILE : (n + 1) * TILE, :]
            halves = []
            for half in range(TILE // HEAD):
                unscaled = jnp.exp2((scores[n * (TILE // HEAD) + half] - peak) * LOG2_SCALE)
                total = total + unscaled
                moved = pltpu.roll(unscaled, 1, 1).astype(jnp.bfloat16)
                halves.append(jnp.concatenate([moved * value_of[k] for k in range(KVH)], axis=0))
            weights = jnp.concatenate(halves, axis=1)
            numer = numer + jnp.dot(weights, tile, preferred_element_type=jnp.float32)
        for shift in (8, 16, 32, 64):
            total = total + pltpu.roll(total, shift, 1)
        out_ref[i, :PROWS, :] = numer.astype(jnp.bfloat16)
        out_ref[i, PROWS:, :] = meta_rows(peak, total)

    def step(s, carry):
        for u in range(UNROLL):
            attend(todo[jnp.minimum(s * UNROLL + u, count - 1)])
        return carry

    lax.fori_loop(0, (count + UNROLL - 1) // UNROLL, step, 0)
    out_first_ref[...] = out_ref[member]
    out_ref[member, :PROWS, :] = no_numer
    out_ref[member, PROWS:, :] = no_meta


def merge_kernel(part_ref, first_ref, out_ref):
    at, lane = iota((HEAD, HEAD), 0), iota((HEAD, HEAD), 1)
    meta = part_ref[:, PROWS:, :].reshape(PLACES * PAD, HEAD)
    meta_first = first_ref[PROWS:, :]
    merged = []
    for k in range(KVH):
        peak_of = ((at % 8 == 2 * k) & (at < 24)).astype(jnp.float32).astype(jnp.bfloat16)
        total_of = ((at % 8 == 2 * k) & (at >= 24) & (at < 48)).astype(jnp.float32).astype(jnp.bfloat16)

        def spread(rows, of):
            return jnp.dot(rows, of, preferred_element_type=jnp.float32)

        peak = spread(meta, peak_of).reshape(PLACES, PAD, HEAD)
        total = spread(meta, total_of).reshape(PLACES, PAD, HEAD)
        peak_first, total_first = spread(meta_first, peak_of), spread(meta_first, total_of)
        top = jnp.maximum(jnp.max(peak, axis=0), peak_first)
        share = jnp.exp2((peak - top[None]) * LOG2_SCALE)
        share_first = jnp.exp2((peak_first - top) * LOG2_SCALE)
        rows = slice(k * PAD, (k + 1) * PAD)
        numer = part_ref[:, rows, :].astype(jnp.float32)
        numer = jnp.sum(share * numer, axis=0) + share_first * first_ref[rows, :].astype(jnp.float32)
        denom = jnp.sum(share * total, axis=0) + share_first * total_first
        merged.append((numer / denom).astype(jnp.bfloat16))
    merged = jnp.concatenate(merged, axis=0)
    out_ref[...] = jnp.dot(
        pad_matrix((QROWS, PROWS), 1), merged, preferred_element_type=jnp.float32
    ).astype(jnp.bfloat16)


def vmem(count):
    return [pl.BlockSpec(memory_space=pltpu.VMEM)] * count


def smem(count):
    return [pl.BlockSpec(memory_space=pltpu.SMEM)] * count


def bf16(*shape):
    return jax.ShapeDtypeStruct(shape, jnp.bfloat16)


def pack(lengths, table, query):
    return pl.pallas_call(
        pack_kernel,
        in_specs=smem(2) + vmem(1),
        out_specs=vmem(2),
        out_shape=[bf16(PLACES, PROWS, HEAD), bf16(PROWS, HEAD)],
    )(lengths, table, query)


def attend_blocks(held, first, lines):
    return pl.pallas_call(
        attend_kernel,
        in_specs=vmem(3),
        out_specs=vmem(2),
        out_shape=[bf16(PLACES, CHUNK, HEAD), bf16(CHUNK, HEAD)],
        scratch_shapes=[
            pltpu.VMEM((PLACES, HEAD), jnp.int32),
            pltpu.SMEM((PLACES, HEAD), jnp.int32),
            pltpu.SMEM((PLACES,), jnp.int32),
            pltpu.SemaphoreType.DMA,
        ],
        compiler_params=pltpu.CompilerParams(vmem_limit_bytes=16 * 2**20),
    )(held, first, lines)


def merge(parts, first):
    return pl.pallas_call(
        merge_kernel,
        in_specs=vmem(2),
        out_specs=vmem(1)[0],
        out_shape=bf16(QROWS, HEAD),
    )(parts, first)


def body(queries, kv_pool, lengths, block_table):
    query = (
        queries.reshape(1, 2, KVH * GROUP, HEAD).transpose(0, 2, 1, 3).reshape(QROWS, HEAD)
    )
    lines = (
        kv_pool.reshape(PLACES, BLOCK, 2, KVH, HEAD)
        .transpose(0, 1, 3, 2, 4)
        .reshape(PLACES, LINES, HEAD)
    )
    lines = pltpu.with_memory_space_constraint(lines, pltpu.VMEM)
    sent, first = pack(lengths, block_table, query)
    first = lax.ppermute(first, "pool", NEXT)
    held = lax.all_to_all(sent, "pool", 0, 0, tiled=True, axis_index_groups=GROUPS)
    parts, part_first = attend_blocks(held, first, lines)
    part_first = lax.ppermute(part_first, "pool", PREVIOUS)
    parts = lax.all_to_all(parts, "pool", 0, 0, tiled=True, axis_index_groups=GROUPS)
    merged = merge(parts, part_first)
    return (
        merged.reshape(1, KVH * GROUP, 2, HEAD)
        .transpose(0, 2, 1, 3)
        .reshape(1, 2, KVH * GROUP * HEAD)
    )


def solution(mesh):
    placed = (P("pool", None, None), P("pool", None, None, None), P("pool"), P("pool"))
    return jax.shard_map(
        body, mesh=mesh, in_specs=placed, out_specs=P("pool", None, None), check_vma=False
    )
```

```python
import jax
import jax.numpy as jnp
from jax import lax
from jax.experimental import pallas as pl
from jax.experimental.pallas import tpu as pltpu
from jax.sharding import PartitionSpec as P

KVH = 4
GROUP = 7
HEAD = 128
BLOCK = 256
PLACES = 32
DEVICES = 128
STRIDE = DEVICES // PLACES
ROWS = 2 * GROUP
PAD = 16
QROWS = KVH * ROWS
PROWS = KVH * PAD
CHUNK = PROWS + PAD
LINES = BLOCK * KVH * 2
TILE = 256
META = ROWS
SCORE_UNROLL = 8
WEIGH_UNROLL = 8
LOG2_SCALE = 1.4426950408889634 / HEAD**0.5
HIDDEN = -(2.0**120)
GROUPS = [[STRIDE * i + r for i in range(PLACES)] for r in range(STRIDE)]
NEXT = [(d, (d + 1) % DEVICES) for d in range(DEVICES)]
PREVIOUS = [((d + 1) % DEVICES, d) for d in range(DEVICES)]


def my_member():
    return lax.axis_index("pool") // STRIDE


def iota(shape, dim):
    return lax.broadcasted_iota(jnp.int32, shape, dim)


def pad_matrix(shape, padded_dim):
    padded, plain = iota(shape, padded_dim), iota(shape, 1 - padded_dim)
    hit = (padded % PAD < ROWS) & (padded // PAD * ROWS + padded % PAD == plain)
    return jnp.where(hit, 1.0, 0.0).astype(jnp.bfloat16)


def split3(x):
    hi = x.astype(jnp.bfloat16).astype(jnp.float32)
    rest = x - hi
    mid = rest.astype(jnp.bfloat16).astype(jnp.float32)
    return hi, mid, rest - mid


def pack_kernel(length_ref, table_ref, query_ref, sent_ref, first_ref):
    member = my_member()
    padded = jnp.dot(
        pad_matrix((PROWS, QROWS), 0),
        query_ref[...].astype(jnp.float32).reshape(QROWS, HEAD).astype(jnp.bfloat16),
        preferred_element_type=jnp.float32,
    )
    length = length_ref[0]
    row, lane = iota((PAD, HEAD), 0), iota((PAD, HEAD), 1)
    is_meta = row == META
    length_lanes = jnp.where(lane == 1, length // 128, jnp.where(lane == 2, length % 128, 0))
    head = padded[:PAD]
    rest = padded[PAD:].astype(jnp.bfloat16)

    def chunk_head(place):
        slot = table_ref[place] % PLACES
        meta = jnp.where(lane == 0, slot, length_lanes).astype(jnp.float32)
        return jnp.where(is_meta, meta, head).astype(jnp.bfloat16)

    for i in range(PLACES):
        sent_ref[i, :PAD, :] = chunk_head(lax.rem(i + PLACES - member, PLACES))
        sent_ref[i, PAD:, :] = rest
    first_ref[:PAD, :] = chunk_head(0)
    first_ref[PAD:, :] = rest


def start_scalars(meta_vmem, meta_smem, sem):
    copy = pltpu.make_async_copy(meta_vmem, meta_smem, sem)
    copy.start()
    return copy


def meta_row(rows):
    rows = rows.astype(jnp.float32)
    rows = jnp.where(iota(rows.shape, rows.ndim - 2) == META, rows, 0.0)
    return jnp.sum(rows, axis=-2, keepdims=rows.ndim == 2).astype(jnp.int32)


def meta_rows(peak, total):
    lane = iota((PAD, HEAD), 1)
    rows = jnp.zeros_like(peak)
    for g, part in enumerate((*split3(peak), *split3(total))):
        rows = jnp.where(lane // 8 == g, part, rows)
    return rows.astype(jnp.bfloat16)


def score(query_ref, lines_ref, score_ref, peak_ref, visible):
    lane = iota((PAD, HEAD), 1)
    head = lane % 8 // 2
    limit = 8 * (visible + iota((PAD, HEAD), 0) % 2)
    query = query_ref[...]
    peak = jnp.full((PAD, HEAD), HIDDEN)
    for n in range(LINES // TILE):
        tile = lines_ref[n * TILE : (n + 1) * TILE, :]
        every = lax.dot_general(
            query, tile, (((1,), (1,)), ((), ())), preferred_element_type=jnp.float32
        )
        for half in range(TILE // HEAD):
            part = every[:, half * HEAD : (half + 1) * HEAD]
            own = part[(KVH - 1) * PAD :]
            for k in range(KVH - 1):
                own = jnp.where(head == k, part[k * PAD : (k + 1) * PAD], own)
            at = n * TILE + half * HEAD
            own = jnp.where(lane < limit - at, own, HIDDEN)
            score_ref[:, at : at + HEAD] = own
            peak = jnp.maximum(peak, own)
    for shift in (8, 16, 32, 64):
        peak = jnp.maximum(peak, pltpu.roll(peak, shift, 1))
    peak_ref[...] = peak


def weigh(lines_ref, score_ref, peak_ref, part_ref):
    lane = iota((PAD, HEAD), 1)
    value_of = [
        jnp.where(lane % 8 == 2 * k + 1, 1.0, 0.0).astype(jnp.bfloat16) for k in range(KVH)
    ]
    peak = peak_ref[...]
    total = jnp.zeros((PAD, HEAD), jnp.float32)
    numer = jnp.zeros((PROWS, HEAD), jnp.float32)
    for n in range(LINES // TILE):
        tile = lines_ref[n * TILE : (n + 1) * TILE, :]
        halves = []
        for half in range(TILE // HEAD):
            at = n * TILE + half * HEAD
            unscaled = jnp.exp2((score_ref[:, at : at + HEAD] - peak) * LOG2_SCALE)
            total = total + unscaled
            moved = pltpu.roll(unscaled, 1, 1).astype(jnp.bfloat16)
            halves.append(jnp.concatenate([moved * value_of[k] for k in range(KVH)], axis=0))
        weights = jnp.concatenate(halves, axis=1)
        numer = numer + jnp.dot(weights, tile, preferred_element_type=jnp.float32)
    for shift in (8, 16, 32, 64):
        total = total + pltpu.roll(total, shift, 1)
    part_ref[:PROWS, :] = numer.astype(jnp.bfloat16)
    part_ref[PROWS:, :] = meta_rows(peak, total)


def first_kernel(
    held_ref, pool_ref, part_ref, meta_vmem, meta_smem, sem, scores, peaks, block, load_sem
):
    meta_vmem[...] = jnp.broadcast_to(meta_row(held_ref[:PAD, :]), (8, HEAD))
    start_scalars(meta_vmem, meta_smem, sem).wait()
    load = pltpu.make_async_copy(pool_ref.at[meta_smem[0, 0]], block, load_sem.at[0])
    load.start()
    load.wait()
    score(held_ref, block, scores, peaks, meta_smem[0, 1] * 128 + meta_smem[0, 2] + 1)
    weigh(block, scores, peaks, part_ref)


def attend_kernel(
    held_ref,
    pool_ref,
    _,
    part_ref,
    meta_vmem,
    meta_smem,
    sem,
    scores,
    peaks,
    blocks,
    load_sems,
    owner_at,
    todo,
):
    def load(slot):
        return pltpu.make_async_copy(pool_ref.at[slot], blocks.at[slot], load_sems.at[slot])

    for slot in range(PLACES):
        load(slot).start()
    member = my_member()
    meta_vmem[...] = meta_row(held_ref[:, :PAD, :])
    copy = start_scalars(meta_vmem, meta_smem, sem)
    lane = iota((PAD, HEAD), 1)
    no_numer = jnp.zeros((PROWS, HEAD), jnp.bfloat16)
    no_meta = meta_rows(jnp.full((PAD, HEAD), HIDDEN), jnp.zeros((PAD, HEAD)))
    for i in range(PLACES):
        part_ref[i, :PROWS, :] = no_numer
        part_ref[i, PROWS:, :] = no_meta
        owner_at[i] = jnp.int32(-1)
    copy.wait()

    def visible(i):
        place = lax.rem(member + PLACES - i, PLACES)
        return meta_smem[i, 1] * 128 + meta_smem[i, 2] + 1 - place * BLOCK

    for i in range(PLACES):
        slot = jnp.where(member == i, PLACES, meta_smem[i, 0])
        owner_at[slot] = jnp.where(visible(i) >= 0, i, -1)
    count = jnp.int32(0)
    for slot in range(PLACES):
        todo[count] = jnp.int32(slot)
        count = count + (owner_at[slot] >= 0).astype(jnp.int32)

    def score_one(slot):
        i = owner_at[slot]
        score(held_ref.at[i], blocks.at[slot], scores.at[slot], peaks.at[slot], visible(i))

    def weigh_one(slot):
        weigh(blocks.at[slot], scores.at[slot], peaks.at[slot], part_ref.at[owner_at[slot]])

    for work, unroll in ((score_one, SCORE_UNROLL), (weigh_one, WEIGH_UNROLL)):
        rest = count % unroll
        whole = count // unroll + (rest > unroll // 2).astype(jnp.int32)

        def several(s, width, work=work, unroll=unroll):
            slots = [todo[jnp.minimum(s * unroll + u, count - 1)] for u in range(width)]
            if work is score_one:
                for u in range(width):

                    @pl.when(s * unroll + u < count)
                    def _(u=u):
                        load(slots[u]).wait()

            for slot in slots:
                work(slot)

        def step(s, carry, unroll=unroll, several=several):
            several(s, unroll)
            return carry

        lax.fori_loop(0, whole, step, 0)

        @pl.when((rest > 0) & (rest <= unroll // 2))
        def _(several=several, whole=whole, unroll=unroll):
            several(whole, unroll // 2)

    for slot in range(PLACES):

        @pl.when(owner_at[slot] < 0)
        def _(slot=slot):
            load(slot).wait()


def merge_kernel(part_ref, first_ref, out_ref):
    at, lane = iota((HEAD, HEAD), 0), iota((HEAD, HEAD), 1)
    meta = part_ref[:, PROWS:, :].reshape(PLACES * PAD, HEAD)
    meta_first = first_ref[PROWS:, :]
    merged = []
    for k in range(KVH):
        peak_of = ((at % 8 == 2 * k) & (at < 24)).astype(jnp.float32).astype(jnp.bfloat16)
        total_of = ((at % 8 == 2 * k) & (at >= 24) & (at < 48)).astype(jnp.float32).astype(jnp.bfloat16)

        def spread(rows, of):
            return jnp.dot(rows, of, preferred_element_type=jnp.float32)

        peak = spread(meta, peak_of).reshape(PLACES, PAD, HEAD)
        total = spread(meta, total_of).reshape(PLACES, PAD, HEAD)
        peak_first, total_first = spread(meta_first, peak_of), spread(meta_first, total_of)
        top = jnp.maximum(jnp.max(peak, axis=0), peak_first)
        share = jnp.exp2((peak - top[None]) * LOG2_SCALE)
        share_first = jnp.exp2((peak_first - top) * LOG2_SCALE)
        rows = slice(k * PAD, (k + 1) * PAD)
        numer = part_ref[:, rows, :].astype(jnp.float32)
        numer = jnp.sum(share * numer, axis=0) + share_first * first_ref[rows, :].astype(jnp.float32)
        denom = jnp.sum(share * total, axis=0) + share_first * total_first
        merged.append((numer / denom).astype(jnp.bfloat16))
    merged = jnp.concatenate(merged, axis=0)
    merged = jnp.dot(
        pad_matrix((QROWS, PROWS), 1), merged, preferred_element_type=jnp.float32
    )
    out_ref[...] = merged.reshape(KVH * GROUP, 2, HEAD).astype(jnp.bfloat16)


def vmem(count):
    return [pl.BlockSpec(memory_space=pltpu.VMEM)] * count


def hbm(count):
    return [pl.BlockSpec(memory_space=pltpu.HBM)] * count


def smem(count):
    return [pl.BlockSpec(memory_space=pltpu.SMEM)] * count


def bf16(*shape):
    return jax.ShapeDtypeStruct(shape, jnp.bfloat16)


def pack(lengths, table, query):
    return pl.pallas_call(
        pack_kernel,
        in_specs=smem(2) + vmem(1),
        out_specs=vmem(2),
        out_shape=[bf16(PLACES, PROWS, HEAD), bf16(PROWS, HEAD)],
        compiler_params=pltpu.CompilerParams(vmem_limit_bytes=8 * 2**20),
    )(lengths, table, query)


def scratch(places, rows):
    return [
        pltpu.VMEM((rows, HEAD), jnp.int32),
        pltpu.SMEM((rows, HEAD), jnp.int32),
        pltpu.SemaphoreType.DMA,
        pltpu.VMEM((*places, PAD, LINES), jnp.float32),
        pltpu.VMEM((*places, PAD, HEAD), jnp.float32),
        pltpu.VMEM((*places, LINES, HEAD), jnp.bfloat16),
        pltpu.SemaphoreType.DMA(places or (1,)),
    ]


def attend_first(held, pool):
    return pl.pallas_call(
        first_kernel,
        in_specs=[*vmem(1), *hbm(1)],
        out_specs=vmem(1)[0],
        out_shape=bf16(CHUNK, HEAD),
        scratch_shapes=scratch((), 8),
        compiler_params=pltpu.CompilerParams(vmem_limit_bytes=8 * 2**20),
    )(held, pool)


def attend_blocks(held, pool, part_first):
    return pl.pallas_call(
        attend_kernel,
        in_specs=[*vmem(1), *hbm(1), pl.BlockSpec(memory_space=pl.ANY)],
        out_specs=vmem(1)[0],
        out_shape=bf16(PLACES, CHUNK, HEAD),
        scratch_shapes=[
            *scratch((PLACES,), PLACES),
            pltpu.SMEM((PLACES + 1,), jnp.int32),
            pltpu.SMEM((PLACES,), jnp.int32),
        ],
        compiler_params=pltpu.CompilerParams(vmem_limit_bytes=32 * 2**20),
    )(held, pool, part_first)


def merge(parts, first):
    return pl.pallas_call(
        merge_kernel,
        in_specs=vmem(2),
        out_specs=vmem(1)[0],
        out_shape=bf16(KVH * GROUP, 2, HEAD),
        compiler_params=pltpu.CompilerParams(vmem_limit_bytes=8 * 2**20),
    )(parts, first)


def body(queries, kv_pool, lengths, block_table):
    query = queries.reshape(2, KVH * GROUP, HEAD).swapaxes(0, 1)
    pool = (
        kv_pool.reshape(PLACES, BLOCK, 2, KVH, HEAD)
        .transpose(0, 1, 3, 2, 4)
        .reshape(PLACES, LINES, HEAD)
    )
    pool = pltpu.with_memory_space_constraint(pool, pltpu.HBM)
    sent, first = pack(lengths, block_table, query)
    first = lax.ppermute(first, "pool", NEXT)
    held = lax.all_to_all(sent, "pool", 0, 0, tiled=True, axis_index_groups=GROUPS)
    part_first = attend_first(first, pool)
    parts = attend_blocks(held, pool, part_first)
    part_first = lax.ppermute(part_first, "pool", PREVIOUS)
    parts = lax.all_to_all(parts, "pool", 0, 0, tiled=True, axis_index_groups=GROUPS)
    merged = merge(parts, part_first)
    return (
        merged.swapaxes(0, 1).reshape(1, 2, KVH * GROUP * HEAD)
    )


def solution(mesh):
    placed = (P("pool", None, None), P("pool", None, None, None), P("pool"), P("pool"))
    return jax.shard_map(
        body, mesh=mesh, in_specs=placed, out_specs=P("pool", None, None), check_vma=False
    )
```

```python
import jax
import jax.numpy as jnp
from jax import lax
from jax.experimental import pallas as pl
from jax.experimental.pallas import tpu as pltpu
from jax.sharding import PartitionSpec as P

KVH = 4
GROUP = 7
HEAD = 128
BLOCK = 256
PLACES = 32
DEVICES = 128
STRIDE = DEVICES // PLACES
ROWS = 2 * GROUP
PAD = 16
QROWS = KVH * ROWS
PROWS = KVH * PAD
CHUNK = PROWS + PAD
LINES = BLOCK * KVH * 2
TILE = 256
META = ROWS
SCORE_UNROLL = 4
WEIGH_UNROLL = 8
LOG2_SCALE = 1.4426950408889634 / HEAD**0.5
HIDDEN = -(2.0**120)
GROUPS = [[STRIDE * i + r for i in range(PLACES)] for r in range(STRIDE)]
NEXT = [(d, (d + 1) % DEVICES) for d in range(DEVICES)]
PREVIOUS = [((d + 1) % DEVICES, d) for d in range(DEVICES)]


def my_member():
    return lax.axis_index("pool") // STRIDE


def iota(shape, dim):
    return lax.broadcasted_iota(jnp.int32, shape, dim)


def pad_matrix(shape, padded_dim):
    padded, plain = iota(shape, padded_dim), iota(shape, 1 - padded_dim)
    hit = (padded % PAD < ROWS) & (padded // PAD * ROWS + padded % PAD == plain)
    return jnp.where(hit, 1.0, 0.0).astype(jnp.bfloat16)


def split3(x):
    hi = x.astype(jnp.bfloat16).astype(jnp.float32)
    rest = x - hi
    mid = rest.astype(jnp.bfloat16).astype(jnp.float32)
    return hi, mid, rest - mid


def pack_kernel(
    length_ref, table_hbm, query_hbm, sent_ref, first_ref, table_ref, query_ref, sems
):
    copies = [
        pltpu.make_async_copy(table_hbm, table_ref, sems.at[0]),
        pltpu.make_async_copy(query_hbm, query_ref, sems.at[1]),
    ]
    for copy in copies:
        copy.start()
    member = my_member()
    for copy in copies:
        copy.wait()
    padded = jnp.dot(
        pad_matrix((PROWS, QROWS), 0),
        query_ref[...].astype(jnp.float32).reshape(QROWS, HEAD).astype(jnp.bfloat16),
        preferred_element_type=jnp.float32,
    )
    length = length_ref[0]
    row, lane = iota((PAD, HEAD), 0), iota((PAD, HEAD), 1)
    is_meta = row == META
    length_lanes = jnp.where(lane == 1, length // 128, jnp.where(lane == 2, length % 128, 0))
    head = padded[:PAD]
    rest = padded[PAD:].astype(jnp.bfloat16)

    def chunk_head(place):
        slot = table_ref[place] % PLACES
        meta = jnp.where(lane == 0, slot, length_lanes).astype(jnp.float32)
        return jnp.where(is_meta, meta, head).astype(jnp.bfloat16)

    for i in range(PLACES):
        sent_ref[i, :PAD, :] = chunk_head(lax.rem(i + PLACES - member, PLACES))
        sent_ref[i, PAD:, :] = rest
    first_ref[:PAD, :] = chunk_head(0)
    first_ref[PAD:, :] = rest


def start_scalars(meta_vmem, meta_smem, sem):
    copy = pltpu.make_async_copy(meta_vmem, meta_smem, sem)
    copy.start()
    return copy


def meta_row(rows):
    rows = rows.astype(jnp.float32)
    rows = jnp.where(iota(rows.shape, rows.ndim - 2) == META, rows, 0.0)
    return jnp.sum(rows, axis=-2, keepdims=rows.ndim == 2).astype(jnp.int32)


def meta_rows(peak, total):
    lane = iota((PAD, HEAD), 1)
    rows = jnp.zeros_like(peak)
    for g, part in enumerate((*split3(peak), *split3(total))):
        rows = jnp.where(lane // 8 == g, part, rows)
    return rows.astype(jnp.bfloat16)


def score(query_ref, lines_ref, score_ref, peak_ref, visible):
    lane = iota((PAD, HEAD), 1)
    head = lane % 8 // 2
    limit = 8 * (visible + iota((PAD, HEAD), 0) % 2)
    query = query_ref[...]
    peak = jnp.full((PAD, HEAD), HIDDEN)
    for n in range(LINES // TILE):
        tile = lines_ref[n * TILE : (n + 1) * TILE, :]
        every = lax.dot_general(
            query, tile, (((1,), (1,)), ((), ())), preferred_element_type=jnp.float32
        )
        for half in range(TILE // HEAD):
            part = every[:, half * HEAD : (half + 1) * HEAD]
            own = part[(KVH - 1) * PAD :]
            for k in range(KVH - 1):
                own = jnp.where(head == k, part[k * PAD : (k + 1) * PAD], own)
            at = n * TILE + half * HEAD
            own = jnp.where(lane < limit - at, own, HIDDEN)
            score_ref[:, at : at + HEAD] = own
            peak = jnp.maximum(peak, own)
    for shift in (8, 16, 32, 64):
        peak = jnp.maximum(peak, pltpu.roll(peak, shift, 1))
    peak_ref[...] = peak


def weigh(lines_ref, score_ref, peak_ref, part_ref):
    lane = iota((PAD, HEAD), 1)
    value_of = [
        jnp.where(lane % 8 == 2 * k + 1, 1.0, 0.0).astype(jnp.bfloat16) for k in range(KVH)
    ]
    peak = peak_ref[...]
    total = jnp.zeros((PAD, HEAD), jnp.float32)
    numer = jnp.zeros((PROWS, HEAD), jnp.float32)
    for n in range(LINES // TILE):
        tile = lines_ref[n * TILE : (n + 1) * TILE, :]
        halves = []
        for half in range(TILE // HEAD):
            at = n * TILE + half * HEAD
            unscaled = jnp.exp2((score_ref[:, at : at + HEAD] - peak) * LOG2_SCALE)
            total = total + unscaled
            moved = pltpu.roll(unscaled, 1, 1).astype(jnp.bfloat16)
            halves.append(jnp.concatenate([moved * value_of[k] for k in range(KVH)], axis=0))
        weights = jnp.concatenate(halves, axis=1)
        numer = numer + jnp.dot(weights, tile, preferred_element_type=jnp.float32)
    for shift in (8, 16, 32, 64):
        total = total + pltpu.roll(total, shift, 1)
    part_ref[:PROWS, :] = numer.astype(jnp.bfloat16)
    part_ref[PROWS:, :] = meta_rows(peak, total)


def first_kernel(
    held_ref, pool_ref, part_ref, meta_vmem, meta_smem, sem, scores, peaks, block, load_sem
):
    meta_vmem[...] = jnp.broadcast_to(meta_row(held_ref[:PAD, :]), (8, HEAD))
    start_scalars(meta_vmem, meta_smem, sem).wait()
    load = pltpu.make_async_copy(pool_ref.at[meta_smem[0, 0]], block, load_sem.at[0])
    load.start()
    load.wait()
    score(held_ref, block, scores, peaks, meta_smem[0, 1] * 128 + meta_smem[0, 2] + 1)
    weigh(block, scores, peaks, part_ref)


def attend_kernel(
    held_ref,
    pool_ref,
    _,
    part_ref,
    meta_vmem,
    meta_smem,
    sem,
    scores,
    peaks,
    blocks,
    load_sems,
    owner_at,
    todo,
):
    def load(slot):
        return pltpu.make_async_copy(pool_ref.at[slot], blocks.at[slot], load_sems.at[slot])

    for slot in range(PLACES):
        load(slot).start()
    member = my_member()
    meta_vmem[...] = meta_row(held_ref[:, :PAD, :])
    copy = start_scalars(meta_vmem, meta_smem, sem)
    lane = iota((PAD, HEAD), 1)
    no_numer = jnp.zeros((PROWS, HEAD), jnp.bfloat16)
    no_meta = meta_rows(jnp.full((PAD, HEAD), HIDDEN), jnp.zeros((PAD, HEAD)))
    for i in range(PLACES):
        part_ref[i, :PROWS, :] = no_numer
        part_ref[i, PROWS:, :] = no_meta
        owner_at[i] = jnp.int32(-1)
    copy.wait()

    def visible(i):
        place = lax.rem(member + PLACES - i, PLACES)
        return meta_smem[i, 1] * 128 + meta_smem[i, 2] + 1 - place * BLOCK

    for i in range(PLACES):
        slot = jnp.where(member == i, PLACES, meta_smem[i, 0])
        owner_at[slot] = jnp.where(visible(i) >= 0, i, -1)
    count = jnp.int32(0)
    for slot in range(PLACES):
        todo[count] = jnp.int32(slot)
        count = count + (owner_at[slot] >= 0).astype(jnp.int32)

    def score_one(slot):
        i = owner_at[slot]
        score(held_ref.at[i], blocks.at[slot], scores.at[slot], peaks.at[slot], visible(i))

    def weigh_one(slot):
        weigh(blocks.at[slot], scores.at[slot], peaks.at[slot], part_ref.at[owner_at[slot]])

    for work, unroll in ((score_one, SCORE_UNROLL), (weigh_one, WEIGH_UNROLL)):
        rest = count % unroll
        whole = count // unroll + (rest > unroll // 2).astype(jnp.int32)

        def several(s, width, work=work, unroll=unroll):
            slots = [todo[jnp.minimum(s * unroll + u, count - 1)] for u in range(width)]
            if work is score_one:
                for u in range(width):

                    @pl.when(s * unroll + u < count)
                    def _(u=u):
                        load(slots[u]).wait()

            for slot in slots:
                work(slot)

        def step(s, carry, unroll=unroll, several=several):
            several(s, unroll)
            return carry

        lax.fori_loop(0, whole, step, 0)

        @pl.when((rest > 0) & (rest <= unroll // 2))
        def _(several=several, whole=whole, unroll=unroll):
            several(whole, unroll // 2)

    for slot in range(PLACES):

        @pl.when(owner_at[slot] < 0)
        def _(slot=slot):
            load(slot).wait()


def merge_kernel(part_ref, first_ref, out_ref):
    at, lane = iota((HEAD, HEAD), 0), iota((HEAD, HEAD), 1)
    meta = part_ref[:, PROWS:, :].reshape(PLACES * PAD, HEAD)
    meta_first = first_ref[PROWS:, :]
    merged = []
    for k in range(KVH):
        peak_of = ((at % 8 == 2 * k) & (at < 24)).astype(jnp.float32).astype(jnp.bfloat16)
        total_of = ((at % 8 == 2 * k) & (at >= 24) & (at < 48)).astype(jnp.float32).astype(jnp.bfloat16)

        def spread(rows, of):
            return jnp.dot(rows, of, preferred_element_type=jnp.float32)

        peak = spread(meta, peak_of).reshape(PLACES, PAD, HEAD)
        total = spread(meta, total_of).reshape(PLACES, PAD, HEAD)
        peak_first, total_first = spread(meta_first, peak_of), spread(meta_first, total_of)
        top = jnp.maximum(jnp.max(peak, axis=0), peak_first)
        share = jnp.exp2((peak - top[None]) * LOG2_SCALE)
        share_first = jnp.exp2((peak_first - top) * LOG2_SCALE)
        rows = slice(k * PAD, (k + 1) * PAD)
        numer = part_ref[:, rows, :].astype(jnp.float32)
        numer = jnp.sum(share * numer, axis=0) + share_first * first_ref[rows, :].astype(jnp.float32)
        denom = jnp.sum(share * total, axis=0) + share_first * total_first
        merged.append((numer / denom).astype(jnp.bfloat16))
    merged = jnp.concatenate(merged, axis=0)
    merged = jnp.dot(
        pad_matrix((QROWS, PROWS), 1), merged, preferred_element_type=jnp.float32
    )
    out_ref[...] = merged.reshape(KVH * GROUP, 2, HEAD).astype(jnp.bfloat16)


def vmem(count):
    return [pl.BlockSpec(memory_space=pltpu.VMEM)] * count


def hbm(count):
    return [pl.BlockSpec(memory_space=pltpu.HBM)] * count


def bf16(*shape):
    return jax.ShapeDtypeStruct(shape, jnp.bfloat16)


def pack(lengths, table, query):
    return pl.pallas_call(
        pack_kernel,
        in_specs=[pl.BlockSpec(memory_space=pltpu.SMEM), *hbm(2)],
        out_specs=vmem(2),
        out_shape=[bf16(PLACES, PROWS, HEAD), bf16(PROWS, HEAD)],
        scratch_shapes=[
            pltpu.SMEM((PLACES,), jnp.int32),
            pltpu.VMEM((KVH * GROUP, 2, HEAD), jnp.bfloat16),
            pltpu.SemaphoreType.DMA((2,)),
        ],
        compiler_params=pltpu.CompilerParams(vmem_limit_bytes=8 * 2**20),
    )(lengths, table, query)


def scratch(places, rows):
    return [
        pltpu.VMEM((rows, HEAD), jnp.int32),
        pltpu.SMEM((rows, HEAD), jnp.int32),
        pltpu.SemaphoreType.DMA,
        pltpu.VMEM((*places, PAD, LINES), jnp.float32),
        pltpu.VMEM((*places, PAD, HEAD), jnp.float32),
        pltpu.VMEM((*places, LINES, HEAD), jnp.bfloat16),
        pltpu.SemaphoreType.DMA(places or (1,)),
    ]


def attend_first(held, pool):
    return pl.pallas_call(
        first_kernel,
        in_specs=[*vmem(1), *hbm(1)],
        out_specs=vmem(1)[0],
        out_shape=bf16(CHUNK, HEAD),
        scratch_shapes=scratch((), 8),
        compiler_params=pltpu.CompilerParams(vmem_limit_bytes=8 * 2**20),
    )(held, pool)


def attend_blocks(held, pool, first):
    return pl.pallas_call(
        attend_kernel,
        in_specs=[*vmem(1), *hbm(1), pl.BlockSpec(memory_space=pl.ANY)],
        out_specs=vmem(1)[0],
        out_shape=bf16(PLACES, CHUNK, HEAD),
        scratch_shapes=[
            *scratch((PLACES,), PLACES),
            pltpu.SMEM((PLACES + 1,), jnp.int32),
            pltpu.SMEM((PLACES,), jnp.int32),
        ],
        compiler_params=pltpu.CompilerParams(vmem_limit_bytes=32 * 2**20),
    )(held, pool, first)


def merge(parts, first):
    return pl.pallas_call(
        merge_kernel,
        in_specs=vmem(2),
        out_specs=vmem(1)[0],
        out_shape=bf16(KVH * GROUP, 2, HEAD),
        compiler_params=pltpu.CompilerParams(vmem_limit_bytes=8 * 2**20),
    )(parts, first)


def body(queries, kv_pool, lengths, block_table):
    query = queries.reshape(2, KVH * GROUP, HEAD).swapaxes(0, 1)
    pool = (
        kv_pool.reshape(PLACES, BLOCK, 2, KVH, HEAD)
        .transpose(0, 1, 3, 2, 4)
        .reshape(PLACES, LINES, HEAD)
    )
    pool = pltpu.with_memory_space_constraint(pool, pltpu.HBM)
    sent, first = pack(
        lengths,
        *(pltpu.with_memory_space_constraint(a, pltpu.HBM) for a in (block_table, query)),
    )
    first = lax.ppermute(first, "pool", NEXT)
    held = lax.all_to_all(sent, "pool", 0, 0, tiled=True, axis_index_groups=GROUPS)
    parts = attend_blocks(held, pool, first)
    part_first = lax.ppermute(attend_first(first, pool), "pool", PREVIOUS)
    parts = lax.all_to_all(parts, "pool", 0, 0, tiled=True, axis_index_groups=GROUPS)
    merged = merge(parts, part_first)
    return (
        merged.swapaxes(0, 1).reshape(1, 2, KVH * GROUP * HEAD)
    )


def solution(mesh):
    placed = (P("pool", None, None), P("pool", None, None, None), P("pool"), P("pool"))
    return jax.shard_map(
        body, mesh=mesh, in_specs=placed, out_specs=P("pool", None, None), check_vma=False
    )
```

```python
import jax
import jax.numpy as jnp
from jax import lax
from jax.experimental import pallas as pl
from jax.experimental.pallas import tpu as pltpu
from jax.sharding import PartitionSpec as P

KVH = 4
GROUP = 7
HEAD = 128
BLOCK = 256
PLACES = 32
DEVICES = 128
STRIDE = DEVICES // PLACES
ROWS = 2 * GROUP
PAD = 16
QROWS = KVH * ROWS
PROWS = KVH * PAD
CHUNK = PROWS + PAD
LINES = BLOCK * KVH * 2
TILE = 256
META = ROWS
SCORE_UNROLL = 4
WEIGH_UNROLL = 8
LOG2_SCALE = 1.4426950408889634 / HEAD**0.5
HIDDEN = -(2.0**120)
GROUPS = [[STRIDE * i + r for i in range(PLACES)] for r in range(STRIDE)]
NEXT = [(d, (d + 1) % DEVICES) for d in range(DEVICES)]
PREVIOUS = [((d + 1) % DEVICES, d) for d in range(DEVICES)]


def my_member():
    return lax.axis_index("pool") // STRIDE


def iota(shape, dim):
    return lax.broadcasted_iota(jnp.int32, shape, dim)


def pad_matrix(shape, padded_dim):
    padded, plain = iota(shape, padded_dim), iota(shape, 1 - padded_dim)
    hit = (padded % PAD < ROWS) & (padded // PAD * ROWS + padded % PAD == plain)
    return jnp.where(hit, 1.0, 0.0).astype(jnp.bfloat16)


def split3(x):
    hi = x.astype(jnp.bfloat16).astype(jnp.float32)
    rest = x - hi
    mid = rest.astype(jnp.bfloat16).astype(jnp.float32)
    return hi, mid, rest - mid


def pack_kernel(
    length_ref, table_hbm, query_hbm, sent_ref, first_ref, table_ref, query_ref, sems
):
    copies = [
        pltpu.make_async_copy(table_hbm, table_ref, sems.at[0]),
        pltpu.make_async_copy(query_hbm, query_ref, sems.at[1]),
    ]
    for copy in copies:
        copy.start()
    member = my_member()
    for copy in copies:
        copy.wait()
    padded = jnp.dot(
        pad_matrix((PROWS, QROWS), 0),
        query_ref[...].astype(jnp.float32).reshape(QROWS, HEAD).astype(jnp.bfloat16),
        preferred_element_type=jnp.float32,
    )
    length = length_ref[0]
    row, lane = iota((PAD, HEAD), 0), iota((PAD, HEAD), 1)
    is_meta = row == META
    length_lanes = jnp.where(lane == 1, length // 128, jnp.where(lane == 2, length % 128, 0))
    head = padded[:PAD]
    rest = padded[PAD:].astype(jnp.bfloat16)

    def chunk_head(place):
        slot = table_ref[place] % PLACES
        meta = jnp.where(lane == 0, slot, length_lanes).astype(jnp.float32)
        return jnp.where(is_meta, meta, head).astype(jnp.bfloat16)

    for i in range(PLACES):
        sent_ref[i, :PAD, :] = chunk_head(lax.rem(i + PLACES - member, PLACES))
        sent_ref[i, PAD:, :] = rest
    first_ref[:PAD, :] = chunk_head(0)
    first_ref[PAD:, :] = rest


def start_scalars(meta_vmem, meta_smem, sem):
    copy = pltpu.make_async_copy(meta_vmem, meta_smem, sem)
    copy.start()
    return copy


def meta_row(rows):
    rows = rows.astype(jnp.float32)
    rows = jnp.where(iota(rows.shape, rows.ndim - 2) == META, rows, 0.0)
    return jnp.sum(rows, axis=-2, keepdims=rows.ndim == 2).astype(jnp.int32)


def meta_rows(peak, total):
    lane = iota((PAD, HEAD), 1)
    rows = jnp.zeros_like(peak)
    for g, part in enumerate((*split3(peak), *split3(total))):
        rows = jnp.where(lane // 8 == g, part, rows)
    return rows.astype(jnp.bfloat16)


def score(query_ref, lines_ref, score_ref, peak_ref, visible):
    lane = iota((PAD, HEAD), 1)
    head = lane % 8 // 2
    limit = 8 * (visible + iota((PAD, HEAD), 0) % 2)
    query = query_ref[...]
    peak = jnp.full((PAD, HEAD), HIDDEN)
    for n in range(LINES // TILE):
        tile = lines_ref[n * TILE : (n + 1) * TILE, :]
        every = lax.dot_general(
            query, tile, (((1,), (1,)), ((), ())), preferred_element_type=jnp.float32
        )
        for half in range(TILE // HEAD):
            part = every[:, half * HEAD : (half + 1) * HEAD]
            own = part[(KVH - 1) * PAD :]
            for k in range(KVH - 1):
                own = jnp.where(head == k, part[k * PAD : (k + 1) * PAD], own)
            at = n * TILE + half * HEAD
            own = jnp.where(lane < limit - at, own, HIDDEN)
            score_ref[:, at : at + HEAD] = own
            peak = jnp.maximum(peak, own)
    for shift in (8, 16, 32, 64):
        peak = jnp.maximum(peak, pltpu.roll(peak, shift, 1))
    peak_ref[...] = peak


def weigh(lines_ref, score_ref, peak_ref, part_ref):
    lane = iota((PAD, HEAD), 1)
    value_of = [
        jnp.where(lane % 8 == 2 * k + 1, 1.0, 0.0).astype(jnp.bfloat16) for k in range(KVH)
    ]
    peak = peak_ref[...]
    total = jnp.zeros((PAD, HEAD), jnp.float32)
    numer = jnp.zeros((PROWS, HEAD), jnp.float32)
    for n in range(LINES // TILE):
        tile = lines_ref[n * TILE : (n + 1) * TILE, :]
        halves = []
        for half in range(TILE // HEAD):
            at = n * TILE + half * HEAD
            unscaled = jnp.exp2((score_ref[:, at : at + HEAD] - peak) * LOG2_SCALE)
            total = total + unscaled
            moved = pltpu.roll(unscaled, 1, 1).astype(jnp.bfloat16)
            halves.append(jnp.concatenate([moved * value_of[k] for k in range(KVH)], axis=0))
        weights = jnp.concatenate(halves, axis=1)
        numer = numer + jnp.dot(weights, tile, preferred_element_type=jnp.float32)
    for shift in (8, 16, 32, 64):
        total = total + pltpu.roll(total, shift, 1)
    part_ref[:PROWS, :] = numer.astype(jnp.bfloat16)
    part_ref[PROWS:, :] = meta_rows(peak, total)


def first_kernel(
    held_ref, pool_ref, part_ref, meta_vmem, meta_smem, sem, scores, peaks, block, load_sem
):
    meta_vmem[...] = jnp.broadcast_to(meta_row(held_ref[:PAD, :]), (8, HEAD))
    start_scalars(meta_vmem, meta_smem, sem).wait()
    load = pltpu.make_async_copy(pool_ref.at[meta_smem[0, 0]], block, load_sem.at[0])
    load.start()
    load.wait()
    score(held_ref, block, scores, peaks, meta_smem[0, 1] * 128 + meta_smem[0, 2] + 1)
    weigh(block, scores, peaks, part_ref)


def empty_kernel(part_ref):
    part_ref[:PROWS, :] = jnp.zeros((PROWS, HEAD), jnp.bfloat16)
    part_ref[PROWS:, :] = meta_rows(jnp.full((PAD, HEAD), HIDDEN), jnp.zeros((PAD, HEAD)))


def attend_kernel(
    held_ref,
    pool_ref,
    empty_ref,
    _,
    part_ref,
    meta_vmem,
    meta_smem,
    sem,
    scores,
    peaks,
    blocks,
    load_sems,
    owner_at,
    todo,
):
    def load(slot):
        return pltpu.make_async_copy(pool_ref.at[slot], blocks.at[slot], load_sems.at[slot])

    for slot in range(PLACES):
        load(slot).start()
    member = my_member()
    meta_vmem[...] = meta_row(held_ref[:, :PAD, :])
    copy = start_scalars(meta_vmem, meta_smem, sem)
    empty = empty_ref[...]
    for i in range(PLACES):
        part_ref[i] = empty
        owner_at[i] = jnp.int32(-1)
    copy.wait()

    def visible(i):
        place = lax.rem(member + PLACES - i, PLACES)
        return meta_smem[i, 1] * 128 + meta_smem[i, 2] + 1 - place * BLOCK

    for i in range(PLACES):
        slot = jnp.where(member == i, PLACES, meta_smem[i, 0])
        owner_at[slot] = jnp.where(visible(i) >= 0, i, -1)
    count = jnp.int32(0)
    for slot in range(PLACES):
        todo[count] = jnp.int32(slot)
        count = count + (owner_at[slot] >= 0).astype(jnp.int32)

    def score_one(slot):
        i = owner_at[slot]
        score(held_ref.at[i], blocks.at[slot], scores.at[slot], peaks.at[slot], visible(i))

    def weigh_one(slot):
        weigh(blocks.at[slot], scores.at[slot], peaks.at[slot], part_ref.at[owner_at[slot]])

    for work, unroll in ((score_one, SCORE_UNROLL), (weigh_one, WEIGH_UNROLL)):
        rest = count % unroll
        whole = count // unroll + (rest > unroll // 2).astype(jnp.int32)

        def several(s, width, work=work, unroll=unroll):
            slots = [todo[jnp.minimum(s * unroll + u, count - 1)] for u in range(width)]
            if work is score_one:
                for u in range(width):

                    @pl.when(s * unroll + u < count)
                    def _(u=u):
                        load(slots[u]).wait()

            for slot in slots:
                work(slot)

        def step(s, carry, unroll=unroll, several=several):
            several(s, unroll)
            return carry

        lax.fori_loop(0, whole, step, 0)

        @pl.when((rest > 0) & (rest <= unroll // 2))
        def _(several=several, whole=whole, unroll=unroll):
            several(whole, unroll // 2)

    for slot in range(PLACES):

        @pl.when(owner_at[slot] < 0)
        def _(slot=slot):
            load(slot).wait()


def merge_kernel(part_ref, first_ref, out_ref):
    at, lane = iota((HEAD, HEAD), 0), iota((HEAD, HEAD), 1)
    meta = part_ref[:, PROWS:, :].reshape(PLACES * PAD, HEAD)
    meta_first = first_ref[PROWS:, :]
    merged = []
    for k in range(KVH):
        peak_of = ((at % 8 == 2 * k) & (at < 24)).astype(jnp.float32).astype(jnp.bfloat16)
        total_of = ((at % 8 == 2 * k) & (at >= 24) & (at < 48)).astype(jnp.float32).astype(jnp.bfloat16)

        def spread(rows, of):
            return jnp.dot(rows, of, preferred_element_type=jnp.float32)

        peak = spread(meta, peak_of).reshape(PLACES, PAD, HEAD)
        total = spread(meta, total_of).reshape(PLACES, PAD, HEAD)
        peak_first, total_first = spread(meta_first, peak_of), spread(meta_first, total_of)
        top = jnp.maximum(jnp.max(peak, axis=0), peak_first)
        share = jnp.exp2((peak - top[None]) * LOG2_SCALE)
        share_first = jnp.exp2((peak_first - top) * LOG2_SCALE)
        rows = slice(k * PAD, (k + 1) * PAD)
        numer = part_ref[:, rows, :].astype(jnp.float32)
        numer = jnp.sum(share * numer, axis=0) + share_first * first_ref[rows, :].astype(jnp.float32)
        denom = jnp.sum(share * total, axis=0) + share_first * total_first
        merged.append((numer / denom).astype(jnp.bfloat16))
    merged = jnp.concatenate(merged, axis=0)
    merged = jnp.dot(
        pad_matrix((QROWS, PROWS), 1), merged, preferred_element_type=jnp.float32
    )
    out_ref[...] = merged.reshape(KVH * GROUP, 2, HEAD).astype(jnp.bfloat16)


def vmem(count):
    return [pl.BlockSpec(memory_space=pltpu.VMEM)] * count


def hbm(count):
    return [pl.BlockSpec(memory_space=pltpu.HBM)] * count


def bf16(*shape):
    return jax.ShapeDtypeStruct(shape, jnp.bfloat16)


def pack(lengths, table, query):
    return pl.pallas_call(
        pack_kernel,
        in_specs=[pl.BlockSpec(memory_space=pltpu.SMEM), *hbm(2)],
        out_specs=vmem(2),
        out_shape=[bf16(PLACES, PROWS, HEAD), bf16(PROWS, HEAD)],
        scratch_shapes=[
            pltpu.SMEM((PLACES,), jnp.int32),
            pltpu.VMEM((KVH * GROUP, 2, HEAD), jnp.bfloat16),
            pltpu.SemaphoreType.DMA((2,)),
        ],
        compiler_params=pltpu.CompilerParams(vmem_limit_bytes=8 * 2**20),
    )(lengths, table, query)


def scratch(places, rows):
    return [
        pltpu.VMEM((rows, HEAD), jnp.int32),
        pltpu.SMEM((rows, HEAD), jnp.int32),
        pltpu.SemaphoreType.DMA,
        pltpu.VMEM((*places, PAD, LINES), jnp.float32),
        pltpu.VMEM((*places, PAD, HEAD), jnp.float32),
        pltpu.VMEM((*places, LINES, HEAD), jnp.bfloat16),
        pltpu.SemaphoreType.DMA(places or (1,)),
    ]


def attend_first(held, pool):
    return pl.pallas_call(
        first_kernel,
        in_specs=[*vmem(1), *hbm(1)],
        out_specs=vmem(1)[0],
        out_shape=bf16(CHUNK, HEAD),
        scratch_shapes=scratch((), 8),
        compiler_params=pltpu.CompilerParams(vmem_limit_bytes=8 * 2**20),
    )(held, pool)


def empty_part():
    return pl.pallas_call(
        empty_kernel,
        out_specs=vmem(1)[0],
        out_shape=bf16(CHUNK, HEAD),
        compiler_params=pltpu.CompilerParams(vmem_limit_bytes=2 * 2**20),
        cost_estimate=pl.CostEstimate(flops=10**10, transcendentals=0, bytes_accessed=2**15),
    )()


def attend_blocks(held, pool, empty, first):
    return pl.pallas_call(
        attend_kernel,
        in_specs=[*vmem(1), *hbm(1), *vmem(1), pl.BlockSpec(memory_space=pl.ANY)],
        out_specs=vmem(1)[0],
        out_shape=bf16(PLACES, CHUNK, HEAD),
        scratch_shapes=[
            *scratch((PLACES,), PLACES),
            pltpu.SMEM((PLACES + 1,), jnp.int32),
            pltpu.SMEM((PLACES,), jnp.int32),
        ],
        compiler_params=pltpu.CompilerParams(vmem_limit_bytes=32 * 2**20),
    )(held, pool, empty, first)


def merge(parts, first):
    return pl.pallas_call(
        merge_kernel,
        in_specs=vmem(2),
        out_specs=vmem(1)[0],
        out_shape=bf16(KVH * GROUP, 2, HEAD),
        compiler_params=pltpu.CompilerParams(vmem_limit_bytes=8 * 2**20),
    )(parts, first)


def body(queries, kv_pool, lengths, block_table):
    query = queries.reshape(2, KVH * GROUP, HEAD).swapaxes(0, 1)
    pool = (
        kv_pool.reshape(PLACES, BLOCK, 2, KVH, HEAD)
        .transpose(0, 1, 3, 2, 4)
        .reshape(PLACES, LINES, HEAD)
    )
    pool = pltpu.with_memory_space_constraint(pool, pltpu.HBM)
    sent, first = pack(
        lengths,
        *(pltpu.with_memory_space_constraint(a, pltpu.HBM) for a in (block_table, query)),
    )
    first = lax.ppermute(first, "pool", NEXT)
    held = lax.all_to_all(sent, "pool", 0, 0, tiled=True, axis_index_groups=GROUPS)
    parts = attend_blocks(held, pool, empty_part(), first)
    part_first = lax.ppermute(attend_first(first, pool), "pool", PREVIOUS)
    parts = lax.all_to_all(parts, "pool", 0, 0, tiled=True, axis_index_groups=GROUPS)
    merged = merge(parts, part_first)
    return (
        merged.swapaxes(0, 1).reshape(1, 2, KVH * GROUP * HEAD)
    )


def solution(mesh):
    placed = (P("pool", None, None), P("pool", None, None, None), P("pool"), P("pool"))
    return jax.shard_map(
        body, mesh=mesh, in_specs=placed, out_specs=P("pool", None, None), check_vma=False
    )
```

```python
import jax
import jax.numpy as jnp
from jax import lax
from jax.experimental import pallas as pl
from jax.experimental.pallas import tpu as pltpu
from jax.sharding import PartitionSpec as P

KVH = 4
GROUP = 7
HEAD = 128
BLOCK = 256
PLACES = 32
DEVICES = 128
STRIDE = DEVICES // PLACES
ROWS = 2 * GROUP
PAD = 16
QROWS = KVH * ROWS
PROWS = KVH * PAD
LINES = BLOCK * KVH * 2
TILE = 256
META = ROWS
SCORE_UNROLL = 4
WEIGH_UNROLL = 8
LOG2_SCALE = 1.4426950408889634 / HEAD**0.5
HIDDEN = -(2.0**120)
GROUPS = [[STRIDE * i + r for i in range(PLACES)] for r in range(STRIDE)]
NEXT = [(d, (d + 1) % DEVICES) for d in range(DEVICES)]
PREVIOUS = [((d + 1) % DEVICES, d) for d in range(DEVICES)]


def my_member():
    return lax.axis_index("pool") // STRIDE


def iota(shape, dim):
    return lax.broadcasted_iota(jnp.int32, shape, dim)


def pad_matrix(shape, padded_dim):
    padded, plain = iota(shape, padded_dim), iota(shape, 1 - padded_dim)
    hit = (padded % PAD < ROWS) & (padded // PAD * ROWS + padded % PAD == plain)
    return jnp.where(hit, 1.0, 0.0).astype(jnp.bfloat16)


def split3(x):
    hi = x.astype(jnp.bfloat16).astype(jnp.float32)
    rest = x - hi
    mid = rest.astype(jnp.bfloat16).astype(jnp.float32)
    return hi, mid, rest - mid


def pack_kernel(
    length_ref, table_hbm, query_hbm, sent_ref, first_ref, table_ref, query_ref, sems
):
    copies = [
        pltpu.make_async_copy(table_hbm, table_ref, sems.at[0]),
        pltpu.make_async_copy(query_hbm, query_ref, sems.at[1]),
    ]
    for copy in copies:
        copy.start()
    member = my_member()
    for copy in copies:
        copy.wait()
    padded = jnp.dot(
        pad_matrix((PROWS, QROWS), 0),
        query_ref[...].astype(jnp.float32).reshape(QROWS, HEAD).astype(jnp.bfloat16),
        preferred_element_type=jnp.float32,
    )
    length = length_ref[0]
    row, lane = iota((PAD, HEAD), 0), iota((PAD, HEAD), 1)
    is_meta = row == META
    length_lanes = jnp.where(lane == 1, length // 128, jnp.where(lane == 2, length % 128, 0))
    head = padded[:PAD]
    rest = padded[PAD:].astype(jnp.bfloat16)

    def chunk_head(place):
        slot = table_ref[place] % PLACES
        meta = jnp.where(lane == 0, slot, length_lanes).astype(jnp.float32)
        return jnp.where(is_meta, meta, head).astype(jnp.bfloat16)

    for i in range(PLACES):
        sent_ref[i, :PAD, :] = chunk_head(lax.rem(i + PLACES - member, PLACES))
        sent_ref[i, PAD:, :] = rest
    first_ref[:PAD, :] = chunk_head(0)
    first_ref[PAD:, :] = rest


def start_scalars(meta_vmem, meta_smem, sem):
    copy = pltpu.make_async_copy(meta_vmem, meta_smem, sem)
    copy.start()
    return copy


def meta_row(rows):
    rows = rows.astype(jnp.float32)
    rows = jnp.where(iota(rows.shape, rows.ndim - 2) == META, rows, 0.0)
    return jnp.sum(rows, axis=-2, keepdims=rows.ndim == 2).astype(jnp.int32)


def store_part(part_ref, numer, peak, total):
    row, lane = iota((PAD, HEAD), 0), iota((PAD, HEAD), 1)
    peak, total = (
        jnp.sum(jnp.where(lane // 8 == row, x, 0.0), axis=0, keepdims=True) for x in (peak, total)
    )
    parts = (*split3(peak), *split3(total))
    for k in range(KVH):
        rows = numer[k * PAD : (k + 1) * PAD]
        for at, part in enumerate(parts[2 * k : 2 * k + 2]):
            rows = jnp.where(row == ROWS + at, part, rows)
        part_ref[k * PAD : (k + 1) * PAD, :] = rows.astype(jnp.bfloat16)


def score(query_ref, lines_ref, score_ref, peak_ref, visible):
    lane = iota((PAD, HEAD), 1)
    head = lane % 8 // 2
    limit = 8 * (visible + iota((PAD, HEAD), 0) % 2)
    query = query_ref[...]
    peak = jnp.full((PAD, HEAD), HIDDEN)
    for n in range(LINES // TILE):
        tile = lines_ref[n * TILE : (n + 1) * TILE, :]
        every = lax.dot_general(
            query, tile, (((1,), (1,)), ((), ())), preferred_element_type=jnp.float32
        )
        for half in range(TILE // HEAD):
            part = every[:, half * HEAD : (half + 1) * HEAD]
            own = part[(KVH - 1) * PAD :]
            for k in range(KVH - 1):
                own = jnp.where(head == k, part[k * PAD : (k + 1) * PAD], own)
            at = n * TILE + half * HEAD
            own = jnp.where(lane < limit - at, own, HIDDEN)
            score_ref[:, at : at + HEAD] = own
            peak = jnp.maximum(peak, own)
    for shift in (8, 16, 32, 64):
        peak = jnp.maximum(peak, pltpu.roll(peak, shift, 1))
    peak_ref[...] = peak


def weigh(lines_ref, score_ref, peak_ref, part_ref):
    lane = iota((PAD, HEAD), 1)
    value_of = [
        jnp.where(lane % 8 == 2 * k + 1, 1.0, 0.0).astype(jnp.bfloat16) for k in range(KVH)
    ]
    peak = peak_ref[...]
    total = jnp.zeros((PAD, HEAD), jnp.float32)
    numer = jnp.zeros((PROWS, HEAD), jnp.float32)
    for n in range(LINES // TILE):
        tile = lines_ref[n * TILE : (n + 1) * TILE, :]
        halves = []
        for half in range(TILE // HEAD):
            at = n * TILE + half * HEAD
            unscaled = jnp.exp2((score_ref[:, at : at + HEAD] - peak) * LOG2_SCALE)
            total = total + unscaled
            moved = pltpu.roll(unscaled, 1, 1).astype(jnp.bfloat16)
            halves.append(jnp.concatenate([moved * value_of[k] for k in range(KVH)], axis=0))
        weights = jnp.concatenate(halves, axis=1)
        numer = numer + jnp.dot(weights, tile, preferred_element_type=jnp.float32)
    for shift in (8, 16, 32, 64):
        total = total + pltpu.roll(total, shift, 1)
    store_part(part_ref, numer, peak, total)


def first_kernel(
    held_ref, pool_ref, part_ref, meta_vmem, meta_smem, sem, scores, peaks, block, load_sem
):
    meta_vmem[...] = jnp.broadcast_to(meta_row(held_ref[:PAD, :]), (8, HEAD))
    start_scalars(meta_vmem, meta_smem, sem).wait()
    load = pltpu.make_async_copy(pool_ref.at[meta_smem[0, 0]], block, load_sem.at[0])
    load.start()
    load.wait()
    score(held_ref, block, scores, peaks, meta_smem[0, 1] * 128 + meta_smem[0, 2] + 1)
    weigh(block, scores, peaks, part_ref)


def attend_kernel(
    held_ref,
    pool_ref,
    _,
    part_ref,
    meta_vmem,
    meta_smem,
    sem,
    scores,
    peaks,
    blocks,
    load_sems,
    owner_at,
    todo,
):
    def load(slot):
        return pltpu.make_async_copy(pool_ref.at[slot], blocks.at[slot], load_sems.at[slot])

    for slot in range(PLACES):
        load(slot).start()
    member = my_member()
    meta_vmem[...] = meta_row(held_ref[:, :PAD, :])
    copy = start_scalars(meta_vmem, meta_smem, sem)
    empty = jnp.where(iota((PROWS, HEAD), 0) == ROWS, HIDDEN, 0.0).astype(jnp.bfloat16)
    for i in range(PLACES):
        part_ref[i] = empty
        owner_at[i] = jnp.int32(-1)
    copy.wait()

    def visible(i):
        place = lax.rem(member + PLACES - i, PLACES)
        return meta_smem[i, 1] * 128 + meta_smem[i, 2] + 1 - place * BLOCK

    for i in range(PLACES):
        slot = jnp.where(member == i, PLACES, meta_smem[i, 0])
        owner_at[slot] = jnp.where(visible(i) >= 0, i, -1)
    count = jnp.int32(0)
    for slot in range(PLACES):
        todo[count] = jnp.int32(slot)
        count = count + (owner_at[slot] >= 0).astype(jnp.int32)

    def score_one(slot):
        i = owner_at[slot]
        score(held_ref.at[i], blocks.at[slot], scores.at[slot], peaks.at[slot], visible(i))

    def weigh_one(slot):
        weigh(blocks.at[slot], scores.at[slot], peaks.at[slot], part_ref.at[owner_at[slot]])

    for work, unroll in ((score_one, SCORE_UNROLL), (weigh_one, WEIGH_UNROLL)):
        rest = count % unroll
        whole = count // unroll + (rest > unroll // 2).astype(jnp.int32)

        def several(s, width, work=work, unroll=unroll):
            slots = [todo[jnp.minimum(s * unroll + u, count - 1)] for u in range(width)]
            if work is score_one:
                for u in range(width):

                    @pl.when(s * unroll + u < count)
                    def _(u=u):
                        load(slots[u]).wait()

            for slot in slots:
                work(slot)

        def step(s, carry, unroll=unroll, several=several):
            several(s, unroll)
            return carry

        lax.fori_loop(0, whole, step, 0)

        @pl.when((rest > 0) & (rest <= unroll // 2))
        def _(several=several, whole=whole, unroll=unroll):
            several(whole, unroll // 2)

    for slot in range(PLACES):

        @pl.when(owner_at[slot] < 0)
        def _(slot=slot):
            load(slot).wait()


def merge_kernel(part_ref, first_ref, out_ref):
    row, lane = iota((PAD, HEAD), 0), iota((PAD, HEAD), 1)

    def heads(ref):
        return [
            ref[..., k * PAD : (k + 1) * PAD, :].astype(jnp.float32) for k in range(KVH)
        ]

    def peak_and_total(numer):
        peak = jnp.where(row >= ROWS, numer[0], 0.0) + jnp.where(row == ROWS, numer[1], 0.0)
        total = jnp.where(row > ROWS, numer[1], 0.0) + jnp.where(row >= ROWS, numer[2], 0.0)
        keep = peak.ndim == 2
        return (jnp.sum(x, axis=-2, keepdims=keep) for x in (peak, total))

    numer, numer_first = heads(part_ref), heads(first_ref)
    peak, total = peak_and_total(numer)
    peak_first, total_first = peak_and_total(numer_first)
    top = jnp.maximum(jnp.max(peak, axis=0, keepdims=True), peak_first)
    share = jnp.exp2((peak - top) * LOG2_SCALE)
    share_first = jnp.exp2((peak_first - top) * LOG2_SCALE)
    denom = jnp.sum(share * total, axis=0, keepdims=True) + share_first * total_first
    share, share_first = share / denom, share_first / denom
    merged = []
    for k in range(KVH):
        own = lane == 8 * row + 2 * k

        def spread(x):
            return jnp.sum(jnp.where(own, x, 0.0), axis=-1, keepdims=True)

        rows = jnp.sum(spread(share[:, None, :]) * numer[k], axis=0)
        rows = rows + spread(share_first) * numer_first[k]
        merged.append(jnp.where(row < ROWS, rows, 0.0).astype(jnp.bfloat16))
    merged = jnp.concatenate(merged, axis=0)
    merged = jnp.dot(
        pad_matrix((QROWS, PROWS), 1), merged, preferred_element_type=jnp.float32
    )
    out_ref[...] = merged.reshape(KVH * GROUP, 2, HEAD).astype(jnp.bfloat16)


def vmem(count):
    return [pl.BlockSpec(memory_space=pltpu.VMEM)] * count


def hbm(count):
    return [pl.BlockSpec(memory_space=pltpu.HBM)] * count


def bf16(*shape):
    return jax.ShapeDtypeStruct(shape, jnp.bfloat16)


def pack(lengths, table, query):
    return pl.pallas_call(
        pack_kernel,
        in_specs=[pl.BlockSpec(memory_space=pltpu.SMEM), *hbm(2)],
        out_specs=vmem(2),
        out_shape=[bf16(PLACES, PROWS, HEAD), bf16(PROWS, HEAD)],
        scratch_shapes=[
            pltpu.SMEM((PLACES,), jnp.int32),
            pltpu.VMEM((KVH * GROUP, 2, HEAD), jnp.bfloat16),
            pltpu.SemaphoreType.DMA((2,)),
        ],
        compiler_params=pltpu.CompilerParams(vmem_limit_bytes=8 * 2**20),
    )(lengths, table, query)


def scratch(places, rows):
    return [
        pltpu.VMEM((rows, HEAD), jnp.int32),
        pltpu.SMEM((rows, HEAD), jnp.int32),
        pltpu.SemaphoreType.DMA,
        pltpu.VMEM((*places, PAD, LINES), jnp.float32),
        pltpu.VMEM((*places, PAD, HEAD), jnp.float32),
        pltpu.VMEM((*places, LINES, HEAD), jnp.bfloat16),
        pltpu.SemaphoreType.DMA(places or (1,)),
    ]


def attend_first(held, pool):
    return pl.pallas_call(
        first_kernel,
        in_specs=[*vmem(1), *hbm(1)],
        out_specs=vmem(1)[0],
        out_shape=bf16(PROWS, HEAD),
        scratch_shapes=scratch((), 8),
        compiler_params=pltpu.CompilerParams(vmem_limit_bytes=8 * 2**20),
    )(held, pool)


def attend_blocks(held, pool, first):
    return pl.pallas_call(
        attend_kernel,
        in_specs=[*vmem(1), *hbm(1), pl.BlockSpec(memory_space=pl.ANY)],
        out_specs=vmem(1)[0],
        out_shape=bf16(PLACES, PROWS, HEAD),
        scratch_shapes=[
            *scratch((PLACES,), PLACES),
            pltpu.SMEM((PLACES + 1,), jnp.int32),
            pltpu.SMEM((PLACES,), jnp.int32),
        ],
        compiler_params=pltpu.CompilerParams(vmem_limit_bytes=32 * 2**20),
    )(held, pool, first)


def merge(parts, first):
    return pl.pallas_call(
        merge_kernel,
        in_specs=vmem(2),
        out_specs=vmem(1)[0],
        out_shape=bf16(KVH * GROUP, 2, HEAD),
        compiler_params=pltpu.CompilerParams(vmem_limit_bytes=8 * 2**20),
    )(parts, first)


def body(queries, kv_pool, lengths, block_table):
    query = queries.reshape(2, KVH * GROUP, HEAD).swapaxes(0, 1)
    pool = (
        kv_pool.reshape(PLACES, BLOCK, 2, KVH, HEAD)
        .transpose(0, 1, 3, 2, 4)
        .reshape(PLACES, LINES, HEAD)
    )
    pool = pltpu.with_memory_space_constraint(pool, pltpu.HBM)
    sent, first = pack(
        lengths,
        *(pltpu.with_memory_space_constraint(a, pltpu.HBM) for a in (block_table, query)),
    )
    first = lax.ppermute(first, "pool", NEXT)
    held = lax.all_to_all(sent, "pool", 0, 0, tiled=True, axis_index_groups=GROUPS)
    parts = attend_blocks(held, pool, first)
    part_first = lax.ppermute(attend_first(first, pool), "pool", PREVIOUS)
    parts = lax.all_to_all(parts, "pool", 0, 0, tiled=True, axis_index_groups=GROUPS)
    merged = merge(parts, part_first)
    return (
        merged.swapaxes(0, 1).reshape(1, 2, KVH * GROUP * HEAD)
    )


def solution(mesh):
    placed = (P("pool", None, None), P("pool", None, None, None), P("pool"), P("pool"))
    return jax.shard_map(
        body, mesh=mesh, in_specs=placed, out_specs=P("pool", None, None), check_vma=False
    )
```

```python
import jax
import jax.numpy as jnp
from jax import lax
from jax.experimental import pallas as pl
from jax.experimental.pallas import tpu as pltpu
from jax.sharding import PartitionSpec as P

KVH = 4
GROUP = 7
HEAD = 128
BLOCK = 256
PLACES = 32
DEVICES = 128
STRIDE = DEVICES // PLACES
ROWS = 2 * GROUP
PAD = 16
QROWS = KVH * ROWS
PROWS = KVH * PAD
LINES = BLOCK * KVH * 2
TILE = 256
META = ROWS
SCORE_UNROLL = 4
WEIGH_UNROLL = 8
LOG2_SCALE = 1.4426950408889634 / HEAD**0.5
HIDDEN = -(2.0**120)
GROUPS = [[STRIDE * i + r for i in range(PLACES)] for r in range(STRIDE)]
NEXT = [(d, (d + 1) % DEVICES) for d in range(DEVICES)]
PREVIOUS = [((d + 1) % DEVICES, d) for d in range(DEVICES)]


def my_member():
    return lax.axis_index("pool") >> 2


def iota(shape, dim):
    return lax.broadcasted_iota(jnp.int32, shape, dim)


def pad_matrix(shape, padded_dim):
    padded, plain = iota(shape, padded_dim), iota(shape, 1 - padded_dim)
    hit = (padded % PAD < ROWS) & (padded // PAD * ROWS + padded % PAD == plain)
    return jnp.where(hit, 1.0, 0.0).astype(jnp.bfloat16)


def split3(x):
    hi = x.astype(jnp.bfloat16).astype(jnp.float32)
    rest = x - hi
    mid = rest.astype(jnp.bfloat16).astype(jnp.float32)
    return hi, mid, rest - mid


def pack_kernel(
    length_ref, table_hbm, query_hbm, sent_ref, first_ref, table_ref, query_ref, sems
):
    copies = [
        pltpu.make_async_copy(table_hbm, table_ref, sems.at[0]),
        pltpu.make_async_copy(query_hbm, query_ref, sems.at[1]),
    ]
    for copy in copies:
        copy.start()
    member = my_member()
    for copy in copies:
        copy.wait()
    padded = jnp.dot(
        pad_matrix((PROWS, QROWS), 0),
        query_ref[...].astype(jnp.float32).reshape(QROWS, HEAD).astype(jnp.bfloat16),
        preferred_element_type=jnp.float32,
    )
    length = length_ref[0]
    row, lane = iota((PAD, HEAD), 0), iota((PAD, HEAD), 1)
    is_meta = row == META
    length_lanes = jnp.where(lane == 1, length >> 7, jnp.where(lane == 2, length & 127, 0))
    head = padded[:PAD]
    rest = padded[PAD:].astype(jnp.bfloat16)

    def chunk_head(place):
        slot = table_ref[place] & (PLACES - 1)
        meta = jnp.where(lane == 0, slot, length_lanes).astype(jnp.float32)
        return jnp.where(is_meta, meta, head).astype(jnp.bfloat16)

    for i in range(PLACES):
        sent_ref[i, :PAD, :] = chunk_head((i + PLACES - member) & (PLACES - 1))
        sent_ref[i, PAD:, :] = rest
    first_ref[:PAD, :] = chunk_head(0)
    first_ref[PAD:, :] = rest


def start_scalars(meta_vmem, meta_smem, sem):
    copy = pltpu.make_async_copy(meta_vmem, meta_smem, sem)
    copy.start()
    return copy


def meta_row(rows):
    rows = rows.astype(jnp.float32)
    rows = jnp.where(iota(rows.shape, rows.ndim - 2) == META, rows, 0.0)
    return jnp.sum(rows, axis=-2, keepdims=rows.ndim == 2).astype(jnp.int32)


def store_part(part_ref, numer, peak, total):
    row, lane = iota((PAD, HEAD), 0), iota((PAD, HEAD), 1)
    peak, total = (
        jnp.sum(jnp.where(lane // 8 == row, x, 0.0), axis=0, keepdims=True) for x in (peak, total)
    )
    parts = (*split3(peak), *split3(total))
    for k in range(KVH):
        rows = numer[k * PAD : (k + 1) * PAD]
        for at, part in enumerate(parts[2 * k : 2 * k + 2]):
            rows = jnp.where(row == ROWS + at, part, rows)
        part_ref[k * PAD : (k + 1) * PAD, :] = rows.astype(jnp.bfloat16)


def score(query_ref, lines_ref, score_ref, peak_ref, visible):
    lane = iota((PAD, HEAD), 1)
    head = lane % 8 // 2
    limit = 8 * (visible + iota((PAD, HEAD), 0) % 2)
    query = query_ref[...]
    peak = jnp.full((PAD, HEAD), HIDDEN)
    for n in range(LINES // TILE):
        tile = lines_ref[n * TILE : (n + 1) * TILE, :]
        every = lax.dot_general(
            query, tile, (((1,), (1,)), ((), ())), preferred_element_type=jnp.float32
        )
        for half in range(TILE // HEAD):
            part = every[:, half * HEAD : (half + 1) * HEAD]
            own = part[(KVH - 1) * PAD :]
            for k in range(KVH - 1):
                own = jnp.where(head == k, part[k * PAD : (k + 1) * PAD], own)
            at = n * TILE + half * HEAD
            own = jnp.where(lane < limit - at, own, HIDDEN)
            score_ref[:, at : at + HEAD] = own
            peak = jnp.maximum(peak, own)
    for shift in (8, 16, 32, 64):
        peak = jnp.maximum(peak, pltpu.roll(peak, shift, 1))
    peak_ref[...] = peak


def weigh(lines_ref, score_ref, peak_ref, part_ref):
    lane = iota((PAD, HEAD), 1)
    value_of = [
        jnp.where(lane % 8 == 2 * k + 1, 1.0, 0.0).astype(jnp.bfloat16) for k in range(KVH)
    ]
    peak = peak_ref[...]
    total = jnp.zeros((PAD, HEAD), jnp.float32)
    numer = jnp.zeros((PROWS, HEAD), jnp.float32)
    for n in range(LINES // TILE):
        tile = lines_ref[n * TILE : (n + 1) * TILE, :]
        halves = []
        for half in range(TILE // HEAD):
            at = n * TILE + half * HEAD
            unscaled = jnp.exp2((score_ref[:, at : at + HEAD] - peak) * LOG2_SCALE)
            total = total + unscaled
            moved = pltpu.roll(unscaled, 1, 1).astype(jnp.bfloat16)
            halves.append(jnp.concatenate([moved * value_of[k] for k in range(KVH)], axis=0))
        weights = jnp.concatenate(halves, axis=1)
        numer = numer + jnp.dot(weights, tile, preferred_element_type=jnp.float32)
    for shift in (8, 16, 32, 64):
        total = total + pltpu.roll(total, shift, 1)
    store_part(part_ref, numer, peak, total)


def first_kernel(
    held_ref, pool_ref, part_ref, meta_vmem, meta_smem, sem, scores, peaks, block, load_sem
):
    meta_vmem[...] = jnp.broadcast_to(meta_row(held_ref[:PAD, :]), (8, HEAD))
    start_scalars(meta_vmem, meta_smem, sem).wait()
    load = pltpu.make_async_copy(pool_ref.at[meta_smem[0, 0]], block, load_sem.at[0])
    load.start()
    load.wait()
    score(held_ref, block, scores, peaks, meta_smem[0, 1] * 128 + meta_smem[0, 2] + 1)
    weigh(block, scores, peaks, part_ref)


def attend_kernel(
    held_ref,
    pool_ref,
    _,
    part_ref,
    meta_vmem,
    meta_smem,
    sem,
    scores,
    peaks,
    blocks,
    load_sems,
    owner_at,
    todo,
):
    def load(slot):
        return pltpu.make_async_copy(pool_ref.at[slot], blocks.at[slot], load_sems.at[slot])

    member = my_member()
    meta_vmem[...] = meta_row(held_ref[:, :PAD, :])
    copy = start_scalars(meta_vmem, meta_smem, sem)
    for slot in range(PLACES):
        load(slot).start()
    empty = jnp.where(iota((PROWS, HEAD), 0) == ROWS, HIDDEN, 0.0).astype(jnp.bfloat16)
    for i in range(PLACES):
        part_ref[i] = empty
        owner_at[i] = jnp.int32(-1)
    copy.wait()

    def visible(i):
        place = (member + PLACES - i) & (PLACES - 1)
        return meta_smem[i, 1] * 128 + meta_smem[i, 2] + 1 - place * BLOCK

    for i in range(PLACES):
        slot = jnp.where(member == i, PLACES, meta_smem[i, 0])
        owner_at[slot] = jnp.where(visible(i) >= 0, i, -1)
    count = jnp.int32(0)
    for slot in range(PLACES):
        todo[count] = jnp.int32(slot)
        count = count + (owner_at[slot] >= 0).astype(jnp.int32)

    def score_one(slot):
        i = owner_at[slot]
        score(held_ref.at[i], blocks.at[slot], scores.at[slot], peaks.at[slot], visible(i))

    def weigh_one(slot):
        weigh(blocks.at[slot], scores.at[slot], peaks.at[slot], part_ref.at[owner_at[slot]])

    for work, unroll in ((score_one, SCORE_UNROLL), (weigh_one, WEIGH_UNROLL)):
        rest = count & (unroll - 1)
        whole = lax.shift_right_logical(count, unroll.bit_length() - 1)
        whole = whole + (rest > unroll // 2).astype(jnp.int32)

        def several(s, width, work=work, unroll=unroll):
            slots = [todo[jnp.minimum(s * unroll + u, count - 1)] for u in range(width)]
            if work is score_one:
                for u in range(width):

                    @pl.when(s * unroll + u < count)
                    def _(u=u):
                        load(slots[u]).wait()

            for slot in slots:
                work(slot)

        def step(s, carry, unroll=unroll, several=several):
            several(s, unroll)
            return carry

        lax.fori_loop(0, whole, step, 0)

        width = unroll // 2
        while width:

            @pl.when((rest > width // 2) & (rest <= width))
            def _(several=several, whole=whole, width=width):
                several(whole, width)

            width //= 2

    for slot in range(PLACES):

        @pl.when(owner_at[slot] < 0)
        def _(slot=slot):
            load(slot).wait()


def merge_kernel(part_ref, first_ref, out_ref):
    row, lane = iota((PAD, HEAD), 0), iota((PAD, HEAD), 1)

    def heads(ref):
        return [
            ref[..., k * PAD : (k + 1) * PAD, :].astype(jnp.float32) for k in range(KVH)
        ]

    def peak_and_total(numer):
        peak = jnp.where(row >= ROWS, numer[0], 0.0) + jnp.where(row == ROWS, numer[1], 0.0)
        total = jnp.where(row > ROWS, numer[1], 0.0) + jnp.where(row >= ROWS, numer[2], 0.0)
        keep = peak.ndim == 2
        return (jnp.sum(x, axis=-2, keepdims=keep) for x in (peak, total))

    numer, numer_first = heads(part_ref), heads(first_ref)
    peak, total = peak_and_total(numer)
    peak_first, total_first = peak_and_total(numer_first)
    top = jnp.maximum(jnp.max(peak, axis=0, keepdims=True), peak_first)
    share = jnp.exp2((peak - top) * LOG2_SCALE)
    share_first = jnp.exp2((peak_first - top) * LOG2_SCALE)
    denom = jnp.sum(share * total, axis=0, keepdims=True) + share_first * total_first
    share, share_first = share / denom, share_first / denom
    merged = []
    for k in range(KVH):
        own = lane == 8 * row + 2 * k

        def spread(x):
            return jnp.sum(jnp.where(own, x, 0.0), axis=-1, keepdims=True)

        rows = jnp.sum(spread(share[:, None, :]) * numer[k], axis=0)
        rows = rows + spread(share_first) * numer_first[k]
        merged.append(jnp.where(row < ROWS, rows, 0.0).astype(jnp.bfloat16))
    merged = jnp.concatenate(merged, axis=0)
    merged = jnp.dot(
        pad_matrix((QROWS, PROWS), 1), merged, preferred_element_type=jnp.float32
    )
    out_ref[...] = merged.reshape(KVH * GROUP, 2, HEAD).astype(jnp.bfloat16)


def vmem(count):
    return [pl.BlockSpec(memory_space=pltpu.VMEM)] * count


def hbm(count):
    return [pl.BlockSpec(memory_space=pltpu.HBM)] * count


def bf16(*shape):
    return jax.ShapeDtypeStruct(shape, jnp.bfloat16)


def pack(lengths, table, query):
    return pl.pallas_call(
        pack_kernel,
        in_specs=[pl.BlockSpec(memory_space=pltpu.SMEM), *hbm(2)],
        out_specs=vmem(2),
        out_shape=[bf16(PLACES, PROWS, HEAD), bf16(PROWS, HEAD)],
        scratch_shapes=[
            pltpu.SMEM((PLACES,), jnp.int32),
            pltpu.VMEM((KVH * GROUP, 2, HEAD), jnp.bfloat16),
            pltpu.SemaphoreType.DMA((2,)),
        ],
        compiler_params=pltpu.CompilerParams(vmem_limit_bytes=8 * 2**20),
    )(lengths, table, query)


def scratch(places, rows):
    return [
        pltpu.VMEM((rows, HEAD), jnp.int32),
        pltpu.SMEM((rows, HEAD), jnp.int32),
        pltpu.SemaphoreType.DMA,
        pltpu.VMEM((*places, PAD, LINES), jnp.float32),
        pltpu.VMEM((*places, PAD, HEAD), jnp.float32),
        pltpu.VMEM((*places, LINES, HEAD), jnp.bfloat16),
        pltpu.SemaphoreType.DMA(places or (1,)),
    ]


def attend_first(held, pool):
    return pl.pallas_call(
        first_kernel,
        in_specs=[*vmem(1), *hbm(1)],
        out_specs=vmem(1)[0],
        out_shape=bf16(PROWS, HEAD),
        scratch_shapes=scratch((), 8),
        compiler_params=pltpu.CompilerParams(vmem_limit_bytes=8 * 2**20),
    )(held, pool)


def attend_blocks(held, pool, first):
    return pl.pallas_call(
        attend_kernel,
        in_specs=[*vmem(1), *hbm(1), pl.BlockSpec(memory_space=pl.ANY)],
        out_specs=vmem(1)[0],
        out_shape=bf16(PLACES, PROWS, HEAD),
        scratch_shapes=[
            *scratch((PLACES,), PLACES),
            pltpu.SMEM((PLACES + 1,), jnp.int32),
            pltpu.SMEM((PLACES,), jnp.int32),
        ],
        compiler_params=pltpu.CompilerParams(vmem_limit_bytes=32 * 2**20),
    )(held, pool, first)


def merge(parts, first):
    return pl.pallas_call(
        merge_kernel,
        in_specs=vmem(2),
        out_specs=vmem(1)[0],
        out_shape=bf16(KVH * GROUP, 2, HEAD),
        compiler_params=pltpu.CompilerParams(vmem_limit_bytes=8 * 2**20),
    )(parts, first)


def body(queries, kv_pool, lengths, block_table):
    query = queries.reshape(2, KVH * GROUP, HEAD).swapaxes(0, 1)
    pool = (
        kv_pool.reshape(PLACES, BLOCK, 2, KVH, HEAD)
        .transpose(0, 1, 3, 2, 4)
        .reshape(PLACES, LINES, HEAD)
    )
    pool = pltpu.with_memory_space_constraint(pool, pltpu.HBM)
    sent, first = pack(
        lengths,
        *(pltpu.with_memory_space_constraint(a, pltpu.HBM) for a in (block_table, query)),
    )
    first = lax.ppermute(first, "pool", NEXT)
    held = lax.all_to_all(sent, "pool", 0, 0, tiled=True, axis_index_groups=GROUPS)
    parts = attend_blocks(held, pool, first)
    part_first = lax.ppermute(attend_first(first, pool), "pool", PREVIOUS)
    parts = lax.all_to_all(parts, "pool", 0, 0, tiled=True, axis_index_groups=GROUPS)
    merged = merge(parts, part_first)
    return (
        merged.swapaxes(0, 1).reshape(1, 2, KVH * GROUP * HEAD)
    )


def solution(mesh):
    placed = (P("pool", None, None), P("pool", None, None, None), P("pool"), P("pool"))
    return jax.shard_map(
        body, mesh=mesh, in_specs=placed, out_specs=P("pool", None, None), check_vma=False
    )
```

```python
import jax
import jax.numpy as jnp
from jax import lax
from jax.experimental import pallas as pl
from jax.experimental.pallas import tpu as pltpu
from jax.sharding import PartitionSpec as P

KVH = 4
GROUP = 7
HEAD = 128
BLOCK = 256
PLACES = 32
DEVICES = 128
STRIDE = DEVICES // PLACES
ROWS = 2 * GROUP
PAD = 16
QROWS = KVH * ROWS
PROWS = KVH * PAD
LINES = BLOCK * KVH * 2
TILE = 256
META = ROWS
EARLY = 12
LOG2_SCALE = 1.4426950408889634 / HEAD**0.5
HIDDEN = -(2.0**120)
GROUPS = [[STRIDE * i + r for i in range(PLACES)] for r in range(STRIDE)]
NEXT = [(d, (d + 1) % DEVICES) for d in range(DEVICES)]
PREVIOUS = [((d + 1) % DEVICES, d) for d in range(DEVICES)]


def my_member():
    return lax.axis_index("pool") >> 2


def iota(shape, dim):
    return lax.broadcasted_iota(jnp.int32, shape, dim)


def pad_matrix(shape, padded_dim):
    padded, plain = iota(shape, padded_dim), iota(shape, 1 - padded_dim)
    hit = (padded % PAD < ROWS) & (padded // PAD * ROWS + padded % PAD == plain)
    return jnp.where(hit, 1.0, 0.0).astype(jnp.bfloat16)


def split3(x):
    hi = x.astype(jnp.bfloat16).astype(jnp.float32)
    rest = x - hi
    mid = rest.astype(jnp.bfloat16).astype(jnp.float32)
    return hi, mid, rest - mid


def pack_kernel(
    length_ref, table_hbm, query_hbm, sent_ref, first_ref, table_ref, query_ref, sems
):
    copies = [
        pltpu.make_async_copy(table_hbm, table_ref, sems.at[0]),
        pltpu.make_async_copy(query_hbm, query_ref, sems.at[1]),
    ]
    for copy in copies:
        copy.start()
    member = my_member()
    for copy in copies:
        copy.wait()
    padded = jnp.dot(
        pad_matrix((PROWS, QROWS), 0),
        query_ref[...].astype(jnp.float32).reshape(QROWS, HEAD).astype(jnp.bfloat16),
        preferred_element_type=jnp.float32,
    )
    length = length_ref[0]
    row, lane = iota((PAD, HEAD), 0), iota((PAD, HEAD), 1)
    is_meta = row == META
    length_lanes = jnp.where(lane == 1, length >> 7, jnp.where(lane == 2, length & 127, 0))
    head = padded[:PAD]
    rest = padded[PAD:].astype(jnp.bfloat16)

    def chunk_head(place):
        slot = table_ref[place] & (PLACES - 1)
        meta = jnp.where(lane == 0, slot, length_lanes).astype(jnp.float32)
        return jnp.where(is_meta, meta, head).astype(jnp.bfloat16)

    for i in range(PLACES):
        sent_ref[i, :PAD, :] = chunk_head((i + PLACES - member) & (PLACES - 1))
        sent_ref[i, PAD:, :] = rest
    first_ref[:PAD, :] = chunk_head(0)
    first_ref[PAD:, :] = rest


def start_scalars(meta_vmem, meta_smem, sem):
    copy = pltpu.make_async_copy(meta_vmem, meta_smem, sem)
    copy.start()
    return copy


def meta_row(rows):
    rows = rows.astype(jnp.float32)
    rows = jnp.where(iota(rows.shape, rows.ndim - 2) == META, rows, 0.0)
    return jnp.sum(rows, axis=-2, keepdims=rows.ndim == 2).astype(jnp.int32)


def store_part(part_ref, numer, peak, total):
    row, lane = iota((PAD, HEAD), 0), iota((PAD, HEAD), 1)
    peak, total = (
        jnp.sum(jnp.where(lane // 8 == row, x, 0.0), axis=0, keepdims=True) for x in (peak, total)
    )
    parts = (*split3(peak), *split3(total))
    for k in range(KVH):
        rows = numer[k * PAD : (k + 1) * PAD]
        for at, part in enumerate(parts[2 * k : 2 * k + 2]):
            rows = jnp.where(row == ROWS + at, part, rows)
        part_ref[k * PAD : (k + 1) * PAD, :] = rows.astype(jnp.bfloat16)


def score(query_ref, lines_ref, score_ref, peak_ref, visible):
    lane = iota((PAD, HEAD), 1)
    head = lane % 8 // 2
    limit = 8 * (visible + iota((PAD, HEAD), 0) % 2)
    query = query_ref[...]
    peak = jnp.full((PAD, HEAD), HIDDEN)
    for n in range(LINES // TILE):
        tile = lines_ref[n * TILE : (n + 1) * TILE, :]
        every = lax.dot_general(
            query, tile, (((1,), (1,)), ((), ())), preferred_element_type=jnp.float32
        )
        for half in range(TILE // HEAD):
            part = every[:, half * HEAD : (half + 1) * HEAD]
            own = part[(KVH - 1) * PAD :]
            for k in range(KVH - 1):
                own = jnp.where(head == k, part[k * PAD : (k + 1) * PAD], own)
            at = n * TILE + half * HEAD
            own = jnp.where(lane < limit - at, own, HIDDEN)
            score_ref[:, at : at + HEAD] = own
            peak = jnp.maximum(peak, own)
    for shift in (8, 16, 32, 64):
        peak = jnp.maximum(peak, pltpu.roll(peak, shift, 1))
    peak_ref[...] = peak


def weigh(lines_ref, score_ref, peak_ref, part_ref):
    lane = iota((PAD, HEAD), 1)
    value_of = [
        jnp.where(lane % 8 == 2 * k + 1, 1.0, 0.0).astype(jnp.bfloat16) for k in range(KVH)
    ]
    peak = peak_ref[...]
    total = jnp.zeros((PAD, HEAD), jnp.float32)
    numer = jnp.zeros((PROWS, HEAD), jnp.float32)
    for n in range(LINES // TILE):
        tile = lines_ref[n * TILE : (n + 1) * TILE, :]
        halves = []
        for half in range(TILE // HEAD):
            at = n * TILE + half * HEAD
            unscaled = jnp.exp2((score_ref[:, at : at + HEAD] - peak) * LOG2_SCALE)
            total = total + unscaled
            moved = pltpu.roll(unscaled, 1, 1).astype(jnp.bfloat16)
            halves.append(jnp.concatenate([moved * value_of[k] for k in range(KVH)], axis=0))
        weights = jnp.concatenate(halves, axis=1)
        numer = numer + jnp.dot(weights, tile, preferred_element_type=jnp.float32)
    for shift in (8, 16, 32, 64):
        total = total + pltpu.roll(total, shift, 1)
    store_part(part_ref, numer, peak, total)


def first_kernel(
    held_ref, pool_ref, part_ref, meta_vmem, meta_smem, sem, scores, peaks, block, load_sem
):
    meta_vmem[...] = jnp.broadcast_to(meta_row(held_ref[:PAD, :]), (8, HEAD))
    start_scalars(meta_vmem, meta_smem, sem).wait()
    load = pltpu.make_async_copy(pool_ref.at[meta_smem[0, 0]], block, load_sem.at[0])
    load.start()
    load.wait()
    score(held_ref, block, scores, peaks, meta_smem[0, 1] * 128 + meta_smem[0, 2] + 1)
    weigh(block, scores, peaks, part_ref)


def attend_kernel(
    held_ref,
    pool_ref,
    _,
    part_ref,
    meta_vmem,
    meta_smem,
    sem,
    scores,
    peaks,
    blocks,
    load_sems,
    owner_at,
    todo,
):
    def load(slot):
        return pltpu.make_async_copy(pool_ref.at[slot], blocks.at[slot], load_sems.at[slot])

    member = my_member()
    meta_vmem[...] = meta_row(held_ref[:, :PAD, :])
    copy = start_scalars(meta_vmem, meta_smem, sem)
    for slot in range(EARLY):
        load(slot).start()
    empty = jnp.where(iota((PROWS, HEAD), 0) == ROWS, HIDDEN, 0.0).astype(jnp.bfloat16)
    for i in range(PLACES):
        part_ref[i] = empty
        owner_at[i] = jnp.int32(-1)
    copy.wait()

    def visible(i):
        place = (member + PLACES - i) & (PLACES - 1)
        return meta_smem[i, 1] * 128 + meta_smem[i, 2] + 1 - place * BLOCK

    for i in range(PLACES):
        slot = jnp.where(member == i, PLACES, meta_smem[i, 0])
        owner_at[slot] = jnp.where(visible(i) >= 0, i, -1)
    count = jnp.int32(0)
    for slot in range(PLACES):
        seen = owner_at[slot] >= 0
        todo[count] = jnp.int32(slot)
        count = count + seen.astype(jnp.int32)
        if slot >= EARLY:

            @pl.when(seen)
            def _(slot=slot):
                load(slot).start()

    def score_one(slot):
        i = owner_at[slot]
        score(held_ref.at[i], blocks.at[slot], scores.at[slot], peaks.at[slot], visible(i))

    def weigh_one(slot):
        weigh(blocks.at[slot], scores.at[slot], peaks.at[slot], part_ref.at[owner_at[slot]])

    for work, narrow in ((score_one, 2), (weigh_one, 0)):

        def several(start, width, work=work):
            slots = [todo[jnp.minimum(start + u, count - 1)] for u in range(width)]
            if work is score_one:
                for u in range(width):

                    @pl.when(start + u < count)
                    def _(u=u):
                        load(slots[u]).wait()

            for slot in slots:
                work(slot)

        def steps(start, width, number, several=several):
            def step(s, carry):
                several(start + s * width, width)
                return carry

            lax.fori_loop(0, number, step, 0)

        start = jnp.int32(0)
        if narrow:
            number = jnp.minimum(count >> 2, narrow)
            steps(start, 4, number)
            start = 4 * number
        rest = (count - start) & 7
        number = ((count - start) >> 3) + (rest > 4).astype(jnp.int32)
        steps(start, 8, number)
        start = start + 8 * number
        for width in (4, 2, 1):

            @pl.when((rest > width // 2) & (rest <= width))
            def _(several=several, start=start, width=width):
                several(start, width)

    for slot in range(EARLY):

        @pl.when(owner_at[slot] < 0)
        def _(slot=slot):
            load(slot).wait()


def merge_kernel(part_ref, first_ref, out_ref):
    row, lane = iota((PAD, HEAD), 0), iota((PAD, HEAD), 1)

    def heads(ref):
        return [
            ref[..., k * PAD : (k + 1) * PAD, :].astype(jnp.float32) for k in range(KVH)
        ]

    def peak_and_total(numer):
        peak = jnp.where(row >= ROWS, numer[0], 0.0) + jnp.where(row == ROWS, numer[1], 0.0)
        total = jnp.where(row > ROWS, numer[1], 0.0) + jnp.where(row >= ROWS, numer[2], 0.0)
        keep = peak.ndim == 2
        return (jnp.sum(x, axis=-2, keepdims=keep) for x in (peak, total))

    numer, numer_first = heads(part_ref), heads(first_ref)
    peak, total = peak_and_total(numer)
    peak_first, total_first = peak_and_total(numer_first)
    top = jnp.maximum(jnp.max(peak, axis=0, keepdims=True), peak_first)
    share = jnp.exp2((peak - top) * LOG2_SCALE)
    share_first = jnp.exp2((peak_first - top) * LOG2_SCALE)
    denom = jnp.sum(share * total, axis=0, keepdims=True) + share_first * total_first
    share, share_first = share / denom, share_first / denom
    merged = []
    for k in range(KVH):
        own = lane == 8 * row + 2 * k

        def spread(x):
            return jnp.sum(jnp.where(own, x, 0.0), axis=-1, keepdims=True)

        rows = jnp.sum(spread(share[:, None, :]) * numer[k], axis=0)
        rows = rows + spread(share_first) * numer_first[k]
        merged.append(jnp.where(row < ROWS, rows, 0.0).astype(jnp.bfloat16))
    merged = jnp.concatenate(merged, axis=0)
    merged = jnp.dot(
        pad_matrix((QROWS, PROWS), 1), merged, preferred_element_type=jnp.float32
    )
    out_ref[...] = merged.reshape(KVH * GROUP, 2, HEAD).astype(jnp.bfloat16)


def vmem(count):
    return [pl.BlockSpec(memory_space=pltpu.VMEM)] * count


def hbm(count):
    return [pl.BlockSpec(memory_space=pltpu.HBM)] * count


def bf16(*shape):
    return jax.ShapeDtypeStruct(shape, jnp.bfloat16)


def pack(lengths, table, query):
    return pl.pallas_call(
        pack_kernel,
        in_specs=[pl.BlockSpec(memory_space=pltpu.SMEM), *hbm(2)],
        out_specs=vmem(2),
        out_shape=[bf16(PLACES, PROWS, HEAD), bf16(PROWS, HEAD)],
        scratch_shapes=[
            pltpu.SMEM((PLACES,), jnp.int32),
            pltpu.VMEM((KVH * GROUP, 2, HEAD), jnp.bfloat16),
            pltpu.SemaphoreType.DMA((2,)),
        ],
        compiler_params=pltpu.CompilerParams(vmem_limit_bytes=8 * 2**20),
    )(lengths, table, query)


def scratch(places, rows):
    return [
        pltpu.VMEM((rows, HEAD), jnp.int32),
        pltpu.SMEM((rows, HEAD), jnp.int32),
        pltpu.SemaphoreType.DMA,
        pltpu.VMEM((*places, PAD, LINES), jnp.float32),
        pltpu.VMEM((*places, PAD, HEAD), jnp.float32),
        pltpu.VMEM((*places, LINES, HEAD), jnp.bfloat16),
        pltpu.SemaphoreType.DMA(places or (1,)),
    ]


def attend_first(held, pool):
    return pl.pallas_call(
        first_kernel,
        in_specs=[*vmem(1), *hbm(1)],
        out_specs=vmem(1)[0],
        out_shape=bf16(PROWS, HEAD),
        scratch_shapes=scratch((), 8),
        compiler_params=pltpu.CompilerParams(vmem_limit_bytes=8 * 2**20),
    )(held, pool)


def attend_blocks(held, pool, first):
    return pl.pallas_call(
        attend_kernel,
        in_specs=[*vmem(1), *hbm(1), pl.BlockSpec(memory_space=pl.ANY)],
        out_specs=vmem(1)[0],
        out_shape=bf16(PLACES, PROWS, HEAD),
        scratch_shapes=[
            *scratch((PLACES,), PLACES),
            pltpu.SMEM((PLACES + 1,), jnp.int32),
            pltpu.SMEM((PLACES,), jnp.int32),
        ],
        compiler_params=pltpu.CompilerParams(vmem_limit_bytes=32 * 2**20),
    )(held, pool, first)


def merge(parts, first):
    return pl.pallas_call(
        merge_kernel,
        in_specs=vmem(2),
        out_specs=vmem(1)[0],
        out_shape=bf16(KVH * GROUP, 2, HEAD),
        compiler_params=pltpu.CompilerParams(vmem_limit_bytes=8 * 2**20),
    )(parts, first)


def body(queries, kv_pool, lengths, block_table):
    query = queries.reshape(2, KVH * GROUP, HEAD).swapaxes(0, 1)
    pool = (
        kv_pool.reshape(PLACES, BLOCK, 2, KVH, HEAD)
        .transpose(0, 1, 3, 2, 4)
        .reshape(PLACES, LINES, HEAD)
    )
    pool = pltpu.with_memory_space_constraint(pool, pltpu.HBM)
    sent, first = pack(
        lengths,
        *(pltpu.with_memory_space_constraint(a, pltpu.HBM) for a in (block_table, query)),
    )
    first = lax.ppermute(first, "pool", NEXT)
    held = lax.all_to_all(sent, "pool", 0, 0, tiled=True, axis_index_groups=GROUPS)
    parts = attend_blocks(held, pool, first)
    part_first = lax.ppermute(attend_first(first, pool), "pool", PREVIOUS)
    parts = lax.all_to_all(parts, "pool", 0, 0, tiled=True, axis_index_groups=GROUPS)
    merged = merge(parts, part_first)
    return (
        merged.swapaxes(0, 1).reshape(1, 2, KVH * GROUP * HEAD)
    )


def solution(mesh):
    placed = (P("pool", None, None), P("pool", None, None, None), P("pool"), P("pool"))
    return jax.shard_map(
        body, mesh=mesh, in_specs=placed, out_specs=P("pool", None, None), check_vma=False
    )
```

```python
import jax
import jax.numpy as jnp
from jax import lax
from jax.experimental import pallas as pl
from jax.experimental.pallas import tpu as pltpu
from jax.sharding import PartitionSpec as P

KVH = 4
GROUP = 7
HEAD = 128
BLOCK = 256
PLACES = 32
DEVICES = 128
STRIDE = DEVICES // PLACES
ROWS = 2 * GROUP
PAD = 16
QROWS = KVH * ROWS
PROWS = KVH * PAD
LINES = BLOCK * KVH * 2
TILE = 256
META = ROWS
EARLY = 8
LOG2_SCALE = 1.4426950408889634 / HEAD**0.5
HIDDEN = -(2.0**120)
GROUPS = [[STRIDE * i + r for i in range(PLACES)] for r in range(STRIDE)]
NEXT = [(d, (d + 1) % DEVICES) for d in range(DEVICES)]
PREVIOUS = [((d + 1) % DEVICES, d) for d in range(DEVICES)]


def my_member():
    return lax.axis_index("pool") >> 2


def iota(shape, dim):
    return lax.broadcasted_iota(jnp.int32, shape, dim)


def pad_matrix(shape, padded_dim):
    padded, plain = iota(shape, padded_dim), iota(shape, 1 - padded_dim)
    hit = (padded % PAD < ROWS) & (padded // PAD * ROWS + padded % PAD == plain)
    return jnp.where(hit, 1.0, 0.0).astype(jnp.bfloat16)


def split3(x):
    hi = x.astype(jnp.bfloat16).astype(jnp.float32)
    rest = x - hi
    mid = rest.astype(jnp.bfloat16).astype(jnp.float32)
    return hi, mid, rest - mid


def pack_kernel(
    length_ref, table_hbm, query_hbm, sent_ref, first_ref, table_ref, query_ref, sems
):
    copies = [
        pltpu.make_async_copy(table_hbm, table_ref, sems.at[0]),
        pltpu.make_async_copy(query_hbm, query_ref, sems.at[1]),
    ]
    for copy in copies:
        copy.start()
    member = my_member()
    for copy in copies:
        copy.wait()
    padded = jnp.dot(
        pad_matrix((PROWS, QROWS), 0),
        query_ref[...].astype(jnp.float32).reshape(QROWS, HEAD).astype(jnp.bfloat16),
        preferred_element_type=jnp.float32,
    )
    length = length_ref[0]
    row, lane = iota((PAD, HEAD), 0), iota((PAD, HEAD), 1)
    is_meta = row == META
    length_lanes = jnp.where(lane == 1, length >> 7, jnp.where(lane == 2, length & 127, 0))
    head = padded[:PAD]
    rest = padded[PAD:].astype(jnp.bfloat16)

    def chunk_head(place):
        slot = table_ref[place] & (PLACES - 1)
        meta = jnp.where(lane == 0, slot, length_lanes).astype(jnp.float32)
        return jnp.where(is_meta, meta, head).astype(jnp.bfloat16)

    for i in range(PLACES):
        sent_ref[i, :PAD, :] = chunk_head((i + PLACES - member) & (PLACES - 1))
        sent_ref[i, PAD:, :] = rest
    first_ref[:PAD, :] = chunk_head(0)
    first_ref[PAD:, :] = rest


def start_scalars(meta_vmem, meta_smem, sem):
    copy = pltpu.make_async_copy(meta_vmem, meta_smem, sem)
    copy.start()
    return copy


def meta_row(rows):
    rows = rows.astype(jnp.float32)
    rows = jnp.where(iota(rows.shape, rows.ndim - 2) == META, rows, 0.0)
    return jnp.sum(rows, axis=-2, keepdims=rows.ndim == 2).astype(jnp.int32)


def store_part(part_ref, numer, peak, total):
    row, lane = iota((PAD, HEAD), 0), iota((PAD, HEAD), 1)
    peak, total = (
        jnp.sum(jnp.where(lane // 8 == row, x, 0.0), axis=0, keepdims=True) for x in (peak, total)
    )
    parts = (*split3(peak), *split3(total))
    for k in range(KVH):
        rows = numer[k * PAD : (k + 1) * PAD]
        for at, part in enumerate(parts[2 * k : 2 * k + 2]):
            rows = jnp.where(row == ROWS + at, part, rows)
        part_ref[k * PAD : (k + 1) * PAD, :] = rows.astype(jnp.bfloat16)


def score(query_ref, lines_ref, score_ref, peak_ref, visible):
    lane = iota((PAD, HEAD), 1)
    head = lane % 8 // 2
    limit = 8 * (visible + iota((PAD, HEAD), 0) % 2)
    query = query_ref[...]
    peak = jnp.full((PAD, HEAD), HIDDEN)
    for n in range(LINES // TILE):
        tile = lines_ref[n * TILE : (n + 1) * TILE, :]
        every = lax.dot_general(
            query, tile, (((1,), (1,)), ((), ())), preferred_element_type=jnp.float32
        )
        for half in range(TILE // HEAD):
            part = every[:, half * HEAD : (half + 1) * HEAD]
            own = part[(KVH - 1) * PAD :]
            for k in range(KVH - 1):
                own = jnp.where(head == k, part[k * PAD : (k + 1) * PAD], own)
            at = n * TILE + half * HEAD
            own = jnp.where(lane < limit - at, own, HIDDEN)
            score_ref[:, at : at + HEAD] = own
            peak = jnp.maximum(peak, own)
    for shift in (8, 16, 32, 64):
        peak = jnp.maximum(peak, pltpu.roll(peak, shift, 1))
    peak_ref[...] = peak


def weigh(lines_ref, score_ref, peak_ref, part_ref):
    lane = iota((PAD, HEAD), 1)
    value_of = [
        jnp.where(lane % 8 == 2 * k + 1, 1.0, 0.0).astype(jnp.bfloat16) for k in range(KVH)
    ]
    peak = peak_ref[...]
    total = jnp.zeros((PAD, HEAD), jnp.float32)
    numer = jnp.zeros((PROWS, HEAD), jnp.float32)
    for n in range(LINES // TILE):
        tile = lines_ref[n * TILE : (n + 1) * TILE, :]
        halves = []
        for half in range(TILE // HEAD):
            at = n * TILE + half * HEAD
            unscaled = jnp.exp2((score_ref[:, at : at + HEAD] - peak) * LOG2_SCALE)
            total = total + unscaled
            moved = pltpu.roll(unscaled, 1, 1).astype(jnp.bfloat16)
            halves.append(jnp.concatenate([moved * value_of[k] for k in range(KVH)], axis=0))
        weights = jnp.concatenate(halves, axis=1)
        numer = numer + jnp.dot(weights, tile, preferred_element_type=jnp.float32)
    for shift in (8, 16, 32, 64):
        total = total + pltpu.roll(total, shift, 1)
    store_part(part_ref, numer, peak, total)


def first_kernel(
    held_ref, pool_ref, part_ref, meta_vmem, meta_smem, sem, scores, peaks, block, load_sem
):
    meta_vmem[...] = jnp.broadcast_to(meta_row(held_ref[:PAD, :]), (8, HEAD))
    start_scalars(meta_vmem, meta_smem, sem).wait()
    load = pltpu.make_async_copy(pool_ref.at[meta_smem[0, 0]], block, load_sem.at[0])
    load.start()
    load.wait()
    score(held_ref, block, scores, peaks, meta_smem[0, 1] * 128 + meta_smem[0, 2] + 1)
    weigh(block, scores, peaks, part_ref)


def attend_kernel(
    held_ref,
    pool_ref,
    _,
    part_ref,
    meta_vmem,
    meta_smem,
    sem,
    scores,
    peaks,
    blocks,
    load_sems,
    owner_at,
    todo,
):
    def load(slot):
        return pltpu.make_async_copy(pool_ref.at[slot], blocks.at[slot], load_sems.at[slot])

    member = my_member()
    meta_vmem[...] = meta_row(held_ref[:, :PAD, :])
    copy = start_scalars(meta_vmem, meta_smem, sem)
    for slot in range(EARLY):
        load(slot).start()
    empty = jnp.where(iota((PROWS, HEAD), 0) == ROWS, HIDDEN, 0.0).astype(jnp.bfloat16)
    for i in range(PLACES):
        part_ref[i] = empty
        owner_at[i] = jnp.int32(-1)
    copy.wait()

    def visible(i):
        place = (member + PLACES - i) & (PLACES - 1)
        return meta_smem[i, 1] * 128 + meta_smem[i, 2] + 1 - place * BLOCK

    for i in range(PLACES):
        slot = jnp.where(member == i, PLACES, meta_smem[i, 0])
        owner_at[slot] = jnp.where(visible(i) >= 0, i, -1)
    count = jnp.int32(0)
    for slot in range(PLACES):
        seen = owner_at[slot] >= 0
        todo[count] = jnp.int32(slot)
        count = count + seen.astype(jnp.int32)
        if slot >= EARLY:

            @pl.when(seen)
            def _(slot=slot):
                load(slot).start()

    def score_one(slot):
        i = owner_at[slot]
        score(held_ref.at[i], blocks.at[slot], scores.at[slot], peaks.at[slot], visible(i))

    def weigh_one(slot):
        weigh(blocks.at[slot], scores.at[slot], peaks.at[slot], part_ref.at[owner_at[slot]])

    for work, narrow in ((score_one, 2), (weigh_one, 0)):

        def several(start, width, work=work):
            slots = [todo[jnp.minimum(start + u, count - 1)] for u in range(width)]
            if work is score_one:
                for u in range(width):

                    @pl.when(start + u < count)
                    def _(u=u):
                        load(slots[u]).wait()

            for slot in slots:
                work(slot)

        def steps(start, width, number, several=several):
            def step(s, carry):
                several(start + s * width, width)
                return carry

            lax.fori_loop(0, number, step, 0)

        start = jnp.int32(0)
        if narrow:
            number = jnp.minimum(count >> 2, narrow)
            steps(start, 4, number)
            start = 4 * number
        rest = (count - start) & 7
        number = ((count - start) >> 3) + (rest > 4).astype(jnp.int32)
        steps(start, 8, number)
        start = start + 8 * number
        for width in (4, 2, 1):

            @pl.when((rest > width // 2) & (rest <= width))
            def _(several=several, start=start, width=width):
                several(start, width)

    for slot in range(EARLY):

        @pl.when(owner_at[slot] < 0)
        def _(slot=slot):
            load(slot).wait()


def merge_kernel(part_ref, first_ref, out_ref):
    row, lane = iota((PAD, HEAD), 0), iota((PAD, HEAD), 1)

    def heads(ref):
        return [
            ref[..., k * PAD : (k + 1) * PAD, :].astype(jnp.float32) for k in range(KVH)
        ]

    def peak_and_total(numer):
        peak = jnp.where(row >= ROWS, numer[0], 0.0) + jnp.where(row == ROWS, numer[1], 0.0)
        total = jnp.where(row > ROWS, numer[1], 0.0) + jnp.where(row >= ROWS, numer[2], 0.0)
        keep = peak.ndim == 2
        return (jnp.sum(x, axis=-2, keepdims=keep) for x in (peak, total))

    numer, numer_first = heads(part_ref), heads(first_ref)
    peak, total = peak_and_total(numer)
    peak_first, total_first = peak_and_total(numer_first)
    top = jnp.maximum(jnp.max(peak, axis=0, keepdims=True), peak_first)
    share = jnp.exp2((peak - top) * LOG2_SCALE)
    share_first = jnp.exp2((peak_first - top) * LOG2_SCALE)
    denom = jnp.sum(share * total, axis=0, keepdims=True) + share_first * total_first
    share, share_first = share / denom, share_first / denom
    merged = []
    for k in range(KVH):
        own = lane == 8 * row + 2 * k

        def spread(x):
            return jnp.sum(jnp.where(own, x, 0.0), axis=-1, keepdims=True)

        rows = jnp.sum(spread(share[:, None, :]) * numer[k], axis=0)
        rows = rows + spread(share_first) * numer_first[k]
        merged.append(jnp.where(row < ROWS, rows, 0.0).astype(jnp.bfloat16))
    merged = jnp.concatenate(merged, axis=0)
    merged = jnp.dot(
        pad_matrix((QROWS, PROWS), 1), merged, preferred_element_type=jnp.float32
    )
    out_ref[...] = merged.reshape(KVH * GROUP, 2, HEAD).astype(jnp.bfloat16)


def vmem(count):
    return [pl.BlockSpec(memory_space=pltpu.VMEM)] * count


def hbm(count):
    return [pl.BlockSpec(memory_space=pltpu.HBM)] * count


def bf16(*shape):
    return jax.ShapeDtypeStruct(shape, jnp.bfloat16)


def pack(lengths, table, query):
    return pl.pallas_call(
        pack_kernel,
        in_specs=[pl.BlockSpec(memory_space=pltpu.SMEM), *hbm(2)],
        out_specs=vmem(2),
        out_shape=[bf16(PLACES, PROWS, HEAD), bf16(PROWS, HEAD)],
        scratch_shapes=[
            pltpu.SMEM((PLACES,), jnp.int32),
            pltpu.VMEM((KVH * GROUP, 2, HEAD), jnp.bfloat16),
            pltpu.SemaphoreType.DMA((2,)),
        ],
        compiler_params=pltpu.CompilerParams(vmem_limit_bytes=8 * 2**20),
    )(lengths, table, query)


def scratch(places, rows):
    return [
        pltpu.VMEM((rows, HEAD), jnp.int32),
        pltpu.SMEM((rows, HEAD), jnp.int32),
        pltpu.SemaphoreType.DMA,
        pltpu.VMEM((*places, PAD, LINES), jnp.float32),
        pltpu.VMEM((*places, PAD, HEAD), jnp.float32),
        pltpu.VMEM((*places, LINES, HEAD), jnp.bfloat16),
        pltpu.SemaphoreType.DMA(places or (1,)),
    ]


def attend_first(held, pool):
    return pl.pallas_call(
        first_kernel,
        in_specs=[*vmem(1), *hbm(1)],
        out_specs=vmem(1)[0],
        out_shape=bf16(PROWS, HEAD),
        scratch_shapes=scratch((), 8),
        compiler_params=pltpu.CompilerParams(vmem_limit_bytes=8 * 2**20),
    )(held, pool)


def attend_blocks(held, pool, first):
    return pl.pallas_call(
        attend_kernel,
        in_specs=[*vmem(1), *hbm(1), pl.BlockSpec(memory_space=pl.ANY)],
        out_specs=vmem(1)[0],
        out_shape=bf16(PLACES, PROWS, HEAD),
        scratch_shapes=[
            *scratch((PLACES,), PLACES),
            pltpu.SMEM((PLACES + 1,), jnp.int32),
            pltpu.SMEM((PLACES,), jnp.int32),
        ],
        compiler_params=pltpu.CompilerParams(vmem_limit_bytes=32 * 2**20),
    )(held, pool, first)


def merge(parts, first):
    return pl.pallas_call(
        merge_kernel,
        in_specs=vmem(2),
        out_specs=vmem(1)[0],
        out_shape=bf16(KVH * GROUP, 2, HEAD),
        compiler_params=pltpu.CompilerParams(vmem_limit_bytes=8 * 2**20),
    )(parts, first)


def body(queries, kv_pool, lengths, block_table):
    query = queries.reshape(2, KVH * GROUP, HEAD).swapaxes(0, 1)
    pool = (
        kv_pool.reshape(PLACES, BLOCK, 2, KVH, HEAD)
        .transpose(0, 1, 3, 2, 4)
        .reshape(PLACES, LINES, HEAD)
    )
    pool = pltpu.with_memory_space_constraint(pool, pltpu.HBM)
    sent, first = pack(
        lengths,
        *(pltpu.with_memory_space_constraint(a, pltpu.HBM) for a in (block_table, query)),
    )
    first = lax.ppermute(first, "pool", NEXT)
    held = lax.all_to_all(sent, "pool", 0, 0, tiled=True, axis_index_groups=GROUPS)
    parts = attend_blocks(held, pool, first)
    part_first = lax.ppermute(attend_first(first, pool), "pool", PREVIOUS)
    parts = lax.all_to_all(parts, "pool", 0, 0, tiled=True, axis_index_groups=GROUPS)
    merged = merge(parts, part_first)
    return (
        merged.swapaxes(0, 1).reshape(1, 2, KVH * GROUP * HEAD)
    )


def solution(mesh):
    placed = (P("pool", None, None), P("pool", None, None, None), P("pool"), P("pool"))
    return jax.shard_map(
        body, mesh=mesh, in_specs=placed, out_specs=P("pool", None, None), check_vma=False
    )
```
